32 devices in a mesh: groups: 1, seq: 8 (over y, x, core), expert: 4 (over z).
Axes of the slice: x: 2, y: 2, z: 4, core: 2. Of those that a mesh axis runs over, the one named last changes fastest.
Arguments:
- queries: bfloat16 [4, 1024, 2048], P(('groups', 'expert'), 'seq'), may hold values from -6 to 6
- keys: bfloat16 [4, 1024, 256], P(('groups', 'expert'), 'seq'), may hold values from -6 to 6
- values: bfloat16 [4, 1024, 256], P(('groups', 'expert'), 'seq'), may hold values from -8 to 8
- document_index: int32 [4, 1024], P(('groups', 'expert')), may hold values from 0 to 3, never falling along the last dimension, each value on 1 to 512 neighbouring positions
- residual: bfloat16 [4, 1024, 2048], P(('groups', 'expert'), 'seq'), may hold values from -4 to 4
- output_projection: bfloat16 [2048, 2048], P(None, 'expert'), may hold values from -0.125 to 0.125
- norm_gain_weight: float32 [2048], replicated, may hold values from 0.5 to 1.5
- routed_experts: int32 [4, 1024, 8], P(('groups', 'expert'), 'seq'), may hold values from 0 to 31, all different within a row; in each aligned block of 128 rows (0 to 127, 128 to 255, ..., all dimensions but the last counted through in order) at most 36 rows name the same one
- router_logits: float32 [4, 1024, 8], P(('groups', 'expert'), 'seq'), may hold values from -12 to 320
- gate_weight: bfloat16 [32, 2048, 768], P(('seq', 'expert')), may hold values from -0.125 to 0.125
- up_weight: bfloat16 [32, 2048, 768], P(('seq', 'expert')), may hold values from -0.125 to 0.125
- down_weight: bfloat16 [32, 768, 2048], P(('seq', 'expert')), may hold values from -0.21875 to 0.21875
- adapter_down: bfloat16 [32, 768, 32], P(('seq', 'expert')), may hold values from -0.21875 to 0.21875
- adapter_up: bfloat16 [32, 32, 2048], P(('seq', 'expert')), may hold values from -1 to 1
- cotangent: bfloat16 [4, 1024, 2048], P(('groups', 'expert'), 'seq'), may hold values from -0.3984375 to 0.3984375
Outputs:
- expert_mixture_output: bfloat16 [4, 1024, 2048], P(('groups', 'expert'), 'seq')
- adapter_down_gradient: float32 [32, 768, 32], P(('groups', 'seq', 'expert'))
- adapter_up_gradient: float32 [32, 32, 2048], P(('groups', 'seq', 'expert'))
- router_logit_gradient: float32 [4, 1024, 8], P(('groups', 'expert'), 'seq')
The draws below stay inside these ranges and needn't reach their ends.
Inputs may be any that keep to these rules, and one draw needn't show every extreme that they name: `routed_experts`: each row names 8 different experts; among the 128 rows of one device (aligned blocks of positions) no expert is named more than 36 times, a bound that some block reaches. `document_index`: never falls along a sequence; at most 4 documents in a sequence.
All inputs are finite; a program needn't handle non-finite values.
Results may differ from the reference program's by a relative error of at most 0.0085.
Values may be sent and summed in bfloat16 or wider, within the bound.
No kernel may reach another device: no remote copies, remote signals or barrier semaphores. Data moves between devices by JAX's collectives and lax.ppermute only.
A program may use at most 128 MiB of HBM per device.

```python
import math
import jax
import jax.numpy as jnp
import numpy as np
from jax import lax

MODEL_DIM = 2048
EXPERT_UNITS = 768
QUERY_HEADS = 16
KEY_VALUE_HEADS = 2
HEAD_SIZE = 128
ADAPTER_RANK = 32
PICKS_PER_TOKEN = 8
DOCS = 4
TOK_DEV = 128
SEQUENCE_LENGTH = 1024
SEQUENCE_COUNT = 4
EXPERT_TOTAL = 32
CAP = 36
N_SEQ = 8
N_EXPERT = 4


def draw_keys(key, part):
    key = jax.random.fold_in(key, 11)
    drawn_values = jnp.clip(jax.random.normal(key, (SEQUENCE_COUNT, SEQUENCE_LENGTH, KEY_VALUE_HEADS * HEAD_SIZE), jnp.float32), -6.0, 6.0)
    return drawn_values.astype(jnp.bfloat16)


def draw_queries(key, part):
    key = jax.random.fold_in(key, 13)
    drawn_values = jnp.clip(jax.random.normal(key, (SEQUENCE_COUNT, SEQUENCE_LENGTH, QUERY_HEADS * HEAD_SIZE), jnp.float32), -6.0, 6.0)
    return drawn_values.astype(jnp.bfloat16)


def draw_router_logits(key, part):
    key = jax.random.fold_in(key, 17)
    key_base = jax.random.fold_in(key, 0)
    background_mask = jnp.clip(2.0 * jax.random.normal(key_base, (SEQUENCE_COUNT, SEQUENCE_LENGTH, PICKS_PER_TOKEN), jnp.float32), -12.0, 12.0)
    drawn_values = background_mask
    return drawn_values


def steps_of(rng, dims, cuts, least, high):
    loudness, own = 1.0, jax.random.fold_in(rng, 6)
    for position, blocks in cuts:
        heights = jnp.exp(jax.random.uniform(jax.random.fold_in(own, position), (blocks,), jnp.float32, least / len(cuts), high / len(cuts)))
        loudness = loudness * jnp.repeat(heights, dims[position] // blocks).reshape([-1 if axis == position else 1 for axis in range(len(dims))])
    return loudness


def length_profile(number_of, total, reach, skew):
    loads = [(1 << 20) // math.isqrt(rank ** skew) + 1 for rank in range(2, number_of + 1)]
    spare, counts = total - reach - (number_of - 1), [1] * (number_of - 1)
    while spare > 0:
        candidates = [i for i in range(number_of - 1) if counts[i] < reach]
        pool, budget = sum([loads[i] for i in candidates]), spare
        for i in candidates:
            extra = min(reach - counts[i], max(1, budget * loads[i] // pool), spare)
            counts[i] = counts[i] + extra
            spare = spare - extra
    return np.array([reach] + counts)


def uneven_parts(stream_key, number_of, total, most, slope):
    if number_of == 2:
        one = jax.random.randint(stream_key, (), max(1, total - most), min(most, total - 1) + 1)
        return jnp.stack([one, total - one])
    sizes = jnp.asarray(length_profile(number_of, total, most, slope), jnp.int32)
    twos = (number_of - 1) // 2
    giver, taker = sizes[1:1 + 2 * twos:2], sizes[2:2 + 2 * twos:2]
    room = jnp.minimum(giver - 1, most - taker)
    moved = jax.random.randint(jax.random.fold_in(stream_key, 1), (twos,), 0, 1 << 20) % (room + 1)
    sizes = sizes.at[1:1 + 2 * twos:2].set(giver - moved).at[2:2 + 2 * twos:2].set(taker + moved)
    return sizes[jax.random.permutation(jax.random.fold_in(stream_key, 2), number_of)]


def shared_out(own_key, own, number, rows, count, top, reach, skew):
    order = jax.random.permutation(own_key, count)
    crowded, common = portions_of(count, rows * top, reach, skew, True), portions_of(count, rows * top, reach, skew, False)
    places = jnp.arange(count)

    def named(lengths, offset_by):
        used = int((lengths > 0).sum())
        fixed = max(1, used // 4)
        moved = fixed + (places - fixed + offset_by * (used - fixed)) % max(1, count - fixed)
        return jnp.zeros((count,), jnp.int32).at[order[jnp.where(places < fixed, places, moved)]].set(jnp.asarray(lengths, jnp.int32))

    lengths = jnp.where(number % 4 == 0, named(crowded, number // 4), named(common, number - number // 4 - 1))
    mixed = jax.random.permutation(jax.random.fold_in(own, 3), count)
    donor, taker = mixed[0:count // 2 * 2:2], mixed[1:count // 2 * 2:2]
    slack = jnp.minimum(lengths[donor] - 1, reach - lengths[taker]) // 2
    slack = jnp.where((donor == order[0]) | (taker == order[0]) | (lengths[taker] == 0), 0, jnp.maximum(slack, 0))
    moved = jax.random.randint(jax.random.fold_in(own, 4), (count // 2,), 0, 1 << 20) % (slack + 1)
    lengths = lengths.at[donor].add(-moved).at[taker].add(moved)
    items = jnp.searchsorted(jnp.cumsum(lengths), jnp.arange(rows * top), side="right").astype(jnp.int32)
    table = items.reshape(top, rows).T
    table = table[jax.random.permutation(jax.random.fold_in(own, 1), rows)]
    offset_by = jax.random.randint(jax.random.fold_in(own, 2), (rows, 1), 0, top)
    return jnp.take_along_axis(table, (jnp.arange(top)[None, :] + offset_by) % top, axis=1)


def portions_of(number_of, total, limit, skew, full):
    loads = [(1 << 20) // math.isqrt(grade ** skew) + 1 for grade in range(1, number_of + 1)]
    largest = limit if full else min(limit, max(-(-total // number_of), total * loads[0] // sum(loads)))
    least = 1 if total - largest >= number_of - 1 else 0
    holding, rest = [largest] + [least] * (number_of - 1), total - largest - least * (number_of - 1)
    while rest > 0:
        movable = [i for i in range(1, number_of) if holding[i] < largest] or [i for i in range(1, number_of) if holding[i] < limit]
        whole, budget = sum([loads[i] for i in movable]), rest
        for i in movable:
            extra = min(limit - holding[i], max(1, budget * loads[i] // whole), rest)
            holding[i] = holding[i] + extra
            rest = rest - extra
    return np.array(holding)


def centred(own_key, shape, scale, bound, cuts=(), held_as=jnp.bfloat16):
    drawn = jax.random.normal(own_key, shape, jnp.float32) * scale
    if len(cuts) > 0:
        drawn = steps_of(own_key, shape, cuts, -0.22, 0.18) * drawn
    return jnp.clip(drawn, min=-bound, max=bound).astype(held_as)


def setup_inputs(seed: int = 0, part: int = 0) -> dict:
    arg_keys = jax.random.split(jax.random.key(seed), 16)
    part_splits = jax.random.split(jax.random.fold_in(arg_keys[15], part), 16)
    queries = draw_queries(jax.random.fold_in(jax.random.fold_in(arg_keys[15], part), 71), part)
    keys = draw_keys(jax.random.fold_in(jax.random.fold_in(arg_keys[15], part), 71), part)
    values = centred(part_splits[2], (SEQUENCE_COUNT, SEQUENCE_LENGTH, KEY_VALUE_HEADS * HEAD_SIZE), 1.5, 8.0, ((0, 4), (1, 8)))
    document_index = jax.vmap(lambda own: jnp.searchsorted(jnp.cumsum(uneven_parts(own, DOCS, SEQUENCE_LENGTH, SEQUENCE_LENGTH // 2, 0)), jnp.arange(SEQUENCE_LENGTH), side="right"))(jax.random.split(part_splits[3], SEQUENCE_COUNT)).reshape((SEQUENCE_COUNT, SEQUENCE_LENGTH)).astype(jnp.int32)
    residual = centred(part_splits[4], (SEQUENCE_COUNT, SEQUENCE_LENGTH, MODEL_DIM), 0.5, 4.0, ((0, 4), (1, 8)))
    output_projection = centred(arg_keys[5], (QUERY_HEADS * HEAD_SIZE, MODEL_DIM), (QUERY_HEADS * HEAD_SIZE) ** -0.5, 0.125, ((1, 4),))
    norm_gain_weight = jnp.clip(1.0 + 0.1 * jax.random.normal(arg_keys[6], (MODEL_DIM,), jnp.float32), 0.5, 1.5)
    routed_experts_keys = jax.random.split(jax.random.fold_in(part_splits[7], 1), SEQUENCE_COUNT * SEQUENCE_LENGTH // TOK_DEV)
    routed_experts_turns = jax.random.permutation(jax.random.fold_in(part_splits[7], 3), SEQUENCE_COUNT * SEQUENCE_LENGTH // TOK_DEV)
    routed_experts = jax.vmap(lambda own, number: shared_out(jax.random.fold_in(part_splits[7], 2), own, number, TOK_DEV, EXPERT_TOTAL, PICKS_PER_TOKEN, CAP, 1))(routed_experts_keys, routed_experts_turns).reshape((SEQUENCE_COUNT, SEQUENCE_LENGTH, PICKS_PER_TOKEN))
    router_logits = draw_router_logits(jax.random.fold_in(jax.random.fold_in(arg_keys[15], part), 71), part)
    gate_weight = centred(arg_keys[9], (EXPERT_TOTAL, MODEL_DIM, EXPERT_UNITS), MODEL_DIM ** -0.5, 0.125, ((0, 32),))
    up_weight = centred(arg_keys[10], (EXPERT_TOTAL, MODEL_DIM, EXPERT_UNITS), MODEL_DIM ** -0.5, 0.125, ((0, 32),))
    down_weight = centred(arg_keys[11], (EXPERT_TOTAL, EXPERT_UNITS, MODEL_DIM), EXPERT_UNITS ** -0.5, 0.21875, ((0, 32),))
    adapter_down = centred(arg_keys[12], (EXPERT_TOTAL, EXPERT_UNITS, ADAPTER_RANK), EXPERT_UNITS ** -0.5, 0.21875, ((0, 32),))
    adapter_up = centred(arg_keys[13], (EXPERT_TOTAL, ADAPTER_RANK, MODEL_DIM), ADAPTER_RANK ** -0.5, 1.0, ((0, 32),))
    cotangent = centred(part_splits[14], (SEQUENCE_COUNT, SEQUENCE_LENGTH, MODEL_DIM), 0.05, 0.3984375, ((0, 4), (1, 8)))
    return {"queries": queries, "keys": keys, "values": values, "document_index": document_index, "residual": residual, "output_projection": output_projection, "norm_gain_weight": norm_gain_weight, "routed_experts": routed_experts, "router_logits": router_logits, "gate_weight": gate_weight, "up_weight": up_weight, "down_weight": down_weight, "adapter_down": adapter_down, "adapter_up": adapter_up, "cotangent": cotangent}


adapter_scale = 2.0
norm_eps = 1e-06

def head_attention(query_rows, key_rows, value_rows, documents):
    scores = jnp.dot(query_rows, key_rows.T, preferred_element_type=jnp.float32) * (1.0 / math.sqrt(HEAD_SIZE))
    positions = jnp.arange(SEQUENCE_LENGTH)
    allowed = (positions[None, :] <= positions[:, None]) & (documents[None, :] == documents[:, None])
    scores = jnp.where(allowed, scores, -jnp.inf)
    weights = jax.nn.softmax(scores, axis=-1).astype(jnp.bfloat16)
    return jnp.dot(weights, value_rows, preferred_element_type=jnp.float32).astype(jnp.bfloat16)

def sequence_attention(packed):
    query_seq, key_sequence, value_sequence, documents = packed
    query_group_size = QUERY_HEADS // KEY_VALUE_HEADS
    query_heads = query_seq.reshape(SEQUENCE_LENGTH, QUERY_HEADS, HEAD_SIZE).transpose(1, 0, 2)
    key_head_rows = jnp.repeat(key_sequence.reshape(SEQUENCE_LENGTH, KEY_VALUE_HEADS, HEAD_SIZE).transpose(1, 0, 2), query_group_size, axis=0)
    value_head_rows = jnp.repeat(value_sequence.reshape(SEQUENCE_LENGTH, KEY_VALUE_HEADS, HEAD_SIZE).transpose(1, 0, 2), query_group_size, axis=0)

    def per_head(triple):
        return head_attention(triple[0], triple[1], triple[2], documents)
    outcome = lax.map(per_head, (query_heads, key_head_rows, value_head_rows))
    return outcome.transpose(1, 0, 2).reshape(SEQUENCE_LENGTH, QUERY_HEADS * HEAD_SIZE)

def expert_forward(layer_inputs, scaled_rows, gate_w, up_w, down_matrix, factor_a, up_factor):
    gate_part = jnp.dot(layer_inputs, gate_w, preferred_element_type=jnp.float32)
    up_part = jnp.dot(layer_inputs, up_w, preferred_element_type=jnp.float32)
    active_rows = (jax.nn.silu(gate_part) * up_part).astype(jnp.bfloat16)
    lowrank_product = jnp.dot(active_rows, factor_a, preferred_element_type=jnp.float32).astype(jnp.bfloat16)
    layer_outputs = (jnp.dot(active_rows, down_matrix, preferred_element_type=jnp.float32) + adapter_scale * jnp.dot(lowrank_product, up_factor, preferred_element_type=jnp.float32)).astype(jnp.bfloat16)
    up_factor_gradient = adapter_scale * jnp.dot(lowrank_product.T, scaled_rows, preferred_element_type=jnp.float32)
    backward_lowrank = jnp.dot(scaled_rows, up_factor.T, preferred_element_type=jnp.float32).astype(jnp.bfloat16)
    down_factor_gradient = adapter_scale * jnp.dot(active_rows.T, backward_lowrank, preferred_element_type=jnp.float32)
    return (layer_outputs, down_factor_gradient, up_factor_gradient)

def reference(queries, keys, values, document_index, residual, output_projection, norm_gain_weight, routed_experts, router_logits, gate_weight, up_weight, down_weight, adapter_down, adapter_up, cotangent):
    attended = lax.map(sequence_attention, (queries, keys, values, document_index))
    merged = attended.reshape(SEQUENCE_COUNT * SEQUENCE_LENGTH, QUERY_HEADS * HEAD_SIZE)
    stream = residual.reshape(SEQUENCE_COUNT * SEQUENCE_LENGTH, MODEL_DIM).astype(jnp.float32) + jnp.dot(merged, output_projection, preferred_element_type=jnp.float32)
    spread = lax.optimization_barrier(jnp.mean(stream * stream, axis=-1, keepdims=True))
    hidden = (stream * lax.rsqrt(spread + norm_eps) * norm_gain_weight).astype(jnp.bfloat16)
    gate_probs = jax.nn.softmax(router_logits.reshape(-1, PICKS_PER_TOKEN), axis=-1)
    pick_ids = routed_experts.reshape(-1)
    flat_gates = gate_probs.reshape(-1)
    upstream = cotangent.reshape(-1, MODEL_DIM)
    total_picks = SEQUENCE_COUNT * SEQUENCE_LENGTH * PICKS_PER_TOKEN
    most_rows = CAP * N_SEQ * N_EXPERT

    def expert_rows(totals, expert_index):
        combined_output, picked_products = totals
        chosen = jnp.nonzero(pick_ids == expert_index, size=most_rows, fill_value=total_picks)[0].astype(jnp.int32)
        usable = chosen < total_picks
        clamped = jnp.minimum(chosen, total_picks - 1)
        token_rows = clamped // PICKS_PER_TOKEN
        gate_rows = jnp.where(usable, flat_gates[clamped], jnp.zeros((), jnp.float32))
        layer_inputs = jnp.where(usable[:, None], hidden[token_rows], jnp.zeros((), jnp.bfloat16))
        cot_rows = upstream[token_rows].astype(jnp.float32)
        scaled_rows = (gate_rows[:, None] * cot_rows).astype(jnp.bfloat16)
        layer_outputs, down_factor_gradient, up_factor_gradient = expert_forward(layer_inputs, scaled_rows, gate_weight[expert_index], up_weight[expert_index], down_weight[expert_index], adapter_down[expert_index], adapter_up[expert_index])
        combined_output = combined_output.at[token_rows].add(gate_rows[:, None] * layer_outputs.astype(jnp.float32))
        row_dots = lax.optimization_barrier(jnp.sum(cot_rows * layer_outputs.astype(jnp.float32), axis=-1))
        picked_products = picked_products.at[chosen].set(row_dots, mode='drop')
        return ((combined_output, picked_products), (down_factor_gradient, up_factor_gradient))
    starting_state = (jnp.zeros((SEQUENCE_COUNT * SEQUENCE_LENGTH, MODEL_DIM), jnp.float32), jnp.zeros((total_picks,), jnp.float32))
    (combined_output, picked_products), (adapter_down_gradient, adapter_up_gradient) = lax.scan(expert_rows, starting_state, jnp.arange(EXPERT_TOTAL, dtype=jnp.int32))
    picked_products = picked_products.reshape(-1, PICKS_PER_TOKEN)
    router_logit_gradient = gate_probs * (picked_products - lax.optimization_barrier(jnp.sum(gate_probs * picked_products, axis=-1, keepdims=True)))
    expert_mixture_output = combined_output.astype(jnp.bfloat16).reshape(SEQUENCE_COUNT, SEQUENCE_LENGTH, MODEL_DIM)
    return (expert_mixture_output, adapter_down_gradient, adapter_up_gradient, router_logit_gradient.reshape(SEQUENCE_COUNT, SEQUENCE_LENGTH, PICKS_PER_TOKEN))
```

```python
import math

import jax
import jax.numpy as jnp
from jax import lax
from jax.experimental import pallas as pl
from jax.experimental.pallas import tpu as pltpu
from jax.sharding import PartitionSpec as P

QUERY_HEADS = 16
KEY_VALUE_HEADS = 2
HEAD_SIZE = 128
PICKS_PER_TOKEN = 8

adapter_scale = 2.0
norm_eps = 1e-06
BF16 = jnp.bfloat16
F32 = jnp.float32


def dot(a, b):
    return jnp.dot(a, b, preferred_element_type=F32)


def dot_t(a, b):
    return lax.dot_general(a, b, (((1,), (1,)), ((), ())), preferred_element_type=F32)


def attend_kernel(start_ref, query_ref, kv_ref, bias_ref, out_ref):
    tokens = query_ref.shape[0]
    window = bias_ref.shape[1]
    start = pl.multiple_of(start_ref[0] * tokens, tokens)
    bias = bias_ref[...]
    group = QUERY_HEADS // KEY_VALUE_HEADS
    width = KEY_VALUE_HEADS * HEAD_SIZE
    factor = math.log2(math.e) / math.sqrt(HEAD_SIZE)
    for kv_head in range(KEY_VALUE_HEADS):
        first = kv_head * HEAD_SIZE
        key_rows = kv_ref[pl.ds(start, window), first : first + HEAD_SIZE]
        value_rows = kv_ref[pl.ds(start, window), width + first : width + first + HEAD_SIZE]
        for pair in range(group // 2):
            at = (kv_head * group + pair * 2) * HEAD_SIZE
            rows = jnp.concatenate(
                [
                    query_ref[:, at : at + HEAD_SIZE],
                    query_ref[:, at + HEAD_SIZE : at + 2 * HEAD_SIZE],
                ],
                axis=0,
            )
            scores = dot_t(rows, key_rows).reshape(2, tokens, window) + bias[None]
            highest = jnp.max(scores, axis=-1, keepdims=True)
            raised = jnp.exp2((scores - highest) * factor)
            total = jnp.sum(raised, axis=-1, keepdims=True)
            mixed = dot(raised.astype(BF16).reshape(2 * tokens, window), value_rows)
            mixed = (mixed.reshape(2, tokens, HEAD_SIZE) / total).astype(BF16)
            out_ref[:, at : at + HEAD_SIZE] = mixed[0]
            out_ref[:, at + HEAD_SIZE : at + 2 * HEAD_SIZE] = mixed[1]


def attend(queries, kv_all, documents):
    tokens = queries.shape[0]
    length = kv_all.shape[0]
    place = lax.axis_index("seq")
    window = min(length, length // 2 + tokens)
    first_block = jnp.clip(place + 1 - window // tokens, 0, (length - window) // tokens)
    mine = place * tokens + jnp.arange(tokens)
    there = first_block * tokens + jnp.arange(window)
    doc_mine = lax.dynamic_slice_in_dim(documents, place * tokens, tokens)
    doc_there = lax.dynamic_slice_in_dim(documents, first_block * tokens, window)
    allowed = (there[None, :] <= mine[:, None]) & (doc_there[None, :] == doc_mine[:, None])
    bias = jnp.where(allowed, 0.0, -jnp.inf).astype(F32)
    return pl.pallas_call(
        attend_kernel,
        out_shape=jax.ShapeDtypeStruct(queries.shape, BF16),
        in_specs=[
            pl.BlockSpec(memory_space=pltpu.SMEM),
            pl.BlockSpec(memory_space=pltpu.VMEM),
            pl.BlockSpec(memory_space=pltpu.VMEM),
            pl.BlockSpec(memory_space=pltpu.VMEM),
        ],
        out_specs=pl.BlockSpec(memory_space=pltpu.VMEM),
        compiler_params=pltpu.CompilerParams(vmem_limit_bytes=32 << 20),
        name="attend",
    )(first_block.reshape(1).astype(jnp.int32), queries, kv_all, bias)


def shards(
    queries,
    keys,
    values,
    document_index,
    residual,
    output_projection,
    norm_gain_weight,
    routed_experts,
    router_logits,
    gate_weight,
    up_weight,
    down_weight,
    adapter_down,
    adapter_up,
    cotangent,
):
    seq_devices = lax.axis_size("seq")
    columns = lax.axis_size("expert")
    column = lax.axis_index("expert")
    tokens = queries.shape[1]
    width = queries.shape[2]
    experts = seq_devices * columns
    rank = adapter_up.shape[1]
    near = columns * tokens

    kv_all = lax.all_gather(
        jnp.concatenate([keys[0], values[0]], axis=1), "seq", axis=0, tiled=True
    )
    gate_probs = jax.nn.softmax(router_logits[0], axis=-1)
    routing = lax.all_gather(
        jnp.concatenate([gate_probs, routed_experts[0].astype(F32)], axis=1),
        "expert",
        axis=0,
        tiled=True,
    )
    projection = lax.all_gather(output_projection, "expert", axis=0)
    up_factors = lax.all_gather(adapter_up[0], "seq", axis=0, tiled=True)
    upstream = lax.all_gather(cotangent[0], "expert", axis=0, tiled=True)

    capacity = columns * (9 * tokens * PICKS_PER_TOKEN // (8 * experts))
    capacity = -(-capacity // 16) * 16
    near_probs = routing[:, :PICKS_PER_TOKEN]
    near_picks = routing[:, PICKS_PER_TOKEN:].astype(jnp.int32)
    plane_experts = jnp.arange(seq_devices) * columns + column
    hits = near_picks[:, :, None] == plane_experts[None, None, :]
    member = jnp.any(hits, axis=1)
    gates = jnp.sum(jnp.where(hits, near_probs[:, :, None], 0.0), axis=1)
    inner = jnp.arange(near)
    lower = (inner[None, :] < inner[:, None]).astype(BF16)
    ranks = dot(lower, member.astype(BF16)).astype(jnp.int32)
    slot = jnp.where(member, ranks, capacity)
    picker = (slot.T[:, None, :] == jnp.arange(capacity)[None, :, None]).reshape(
        seq_devices * capacity, near
    )
    onehot = picker.astype(BF16)
    weighted = (
        jnp.where(picker.reshape(seq_devices, capacity, near), gates.T[:, None, :], 0.0)
        .astype(BF16)
        .reshape(seq_devices * capacity, near)
    )

    back_all = dot_t(upstream, up_factors).reshape(near, seq_devices, rank)
    back_all = (back_all * gates[:, :, None]).astype(BF16)
    back_slots = jnp.einsum(
        "jct,tjr->jcr",
        onehot.reshape(seq_devices, capacity, near),
        back_all,
        preferred_element_type=F32,
    ).astype(BF16)
    back_low = lax.all_to_all(back_slots, "seq", split_axis=0, concat_axis=0, tiled=True)
    back_low = back_low.reshape(seq_devices * capacity, rank)
    upstream_slots = dot(onehot, upstream).astype(BF16)

    attended = attend(queries[0], kv_all, document_index[0])
    projected = jnp.einsum("tk,zkn->tzn", attended, projection, preferred_element_type=F32)
    stream = residual[0].astype(F32) + projected.reshape(tokens, width)
    spread = jnp.mean(stream * stream, axis=-1, keepdims=True)
    hidden = (stream * lax.rsqrt(spread + norm_eps) * norm_gain_weight).astype(BF16)

    hidden_near = lax.all_gather(hidden, "expert", axis=0, tiled=True)
    sent = dot(onehot, hidden_near).astype(BF16).reshape(seq_devices, capacity, width)
    rows = lax.all_to_all(sent, "seq", split_axis=0, concat_axis=0, tiled=True)
    rows = rows.reshape(seq_devices * capacity, width)

    gate_part = dot(rows, gate_weight[0])
    up_part = dot(rows, up_weight[0])
    active = (jax.nn.silu(gate_part) * up_part).astype(BF16)
    low_rank = dot(active, adapter_down[0]).astype(BF16)
    outputs = (dot(active, down_weight[0]) + adapter_scale * dot(low_rank, adapter_up[0])).astype(
        BF16
    )
    down_factor_gradient = adapter_scale * lax.dot_general(
        active, back_low, (((0,), (0,)), ((), ())), preferred_element_type=F32
    )
    low_near = lax.all_to_all(
        low_rank.reshape(seq_devices, capacity, rank), "seq", split_axis=0, concat_axis=0, tiled=True
    )
    returned = lax.all_to_all(
        outputs.reshape(seq_devices, capacity, width),
        "seq",
        split_axis=0,
        concat_axis=0,
        tiled=True,
    ).reshape(seq_devices * capacity, width)

    low_weighted = jnp.einsum(
        "jct,jcr->jrt",
        weighted.reshape(seq_devices, capacity, near),
        low_near,
        preferred_element_type=F32,
    ).astype(BF16)
    up_parts = dot(low_weighted.reshape(seq_devices * rank, near), upstream)
    up_factor_gradient = adapter_scale * lax.psum_scatter(
        up_parts, "seq", scatter_dimension=0, tiled=True
    )

    combined = lax.dot_general(
        weighted, returned, (((0,), (0,)), ((), ())), preferred_element_type=F32
    )
    slot_dots = jnp.sum(returned.astype(F32) * upstream_slots.astype(F32), axis=-1)
    plane_dots = jnp.sum(
        jnp.where(
            picker.reshape(seq_devices, capacity, near),
            slot_dots.reshape(seq_devices, capacity, 1),
            0.0,
        ),
        axis=1,
    )
    all_dots = lax.all_to_all(
        plane_dots.T.reshape(columns, tokens, seq_devices),
        "expert",
        split_axis=0,
        concat_axis=0,
        tiled=True,
    )
    combined_output = lax.psum_scatter(
        combined.astype(BF16), "expert", scatter_dimension=0, tiled=True
    )
    by_expert = all_dots.transpose(1, 2, 0).reshape(tokens, experts)
    own_hits = routed_experts[0][:, :, None] == jnp.arange(experts)[None, None, :]
    picked_products = jnp.sum(jnp.where(own_hits, by_expert[:, None, :], 0.0), axis=-1)
    router_logit_gradient = gate_probs * (
        picked_products - jnp.sum(gate_probs * picked_products, axis=-1, keepdims=True)
    )
    return (
        combined_output.astype(BF16)[None],
        down_factor_gradient[None],
        up_factor_gradient[None],
        router_logit_gradient[None],
    )


def solution(mesh):
    return jax.shard_map(
        shards,
        mesh=mesh,
        in_specs=(
            P(("groups", "expert"), "seq", None),
            P(("groups", "expert"), "seq", None),
            P(("groups", "expert"), "seq", None),
            P(("groups", "expert"), None),
            P(("groups", "expert"), "seq", None),
            P(None, "expert"),
            P(),
            P(("groups", "expert"), "seq", None),
            P(("groups", "expert"), "seq", None),
            P(("seq", "expert"), None, None),
            P(("seq", "expert"), None, None),
            P(("seq", "expert"), None, None),
            P(("seq", "expert"), None, None),
            P(("seq", "expert"), None, None),
            P(("groups", "expert"), "seq", None),
        ),
        out_specs=(
            P(("groups", "expert"), "seq", None),
            P(("groups", "seq", "expert"), None, None),
            P(("groups", "seq", "expert"), None, None),
            P(("groups", "expert"), "seq", None),
        ),
        check_vma=False,
    )
```

```python
import math

import jax
import jax.numpy as jnp
from jax import lax
from jax.experimental import pallas as pl
from jax.experimental.pallas import tpu as pltpu
from jax.sharding import PartitionSpec as P

QUERY_HEADS = 16
KEY_VALUE_HEADS = 2
HEAD_SIZE = 128
PICKS_PER_TOKEN = 8

adapter_scale = 2.0
norm_eps = 1e-06
BF16 = jnp.bfloat16
F32 = jnp.float32


def dot(a, b):
    return jnp.dot(a, b, preferred_element_type=F32)


def dot_t(a, b):
    return lax.dot_general(a, b, (((1,), (1,)), ((), ())), preferred_element_type=F32)


def attend_kernel(start_ref, query_ref, kv_ref, bias_ref, *refs):
    out_ref = refs[-1]
    tokens = query_ref.shape[0]
    window = bias_ref.shape[1]
    start = pl.multiple_of(start_ref[0] * tokens, tokens)
    bias = bias_ref[...]
    group = QUERY_HEADS // KEY_VALUE_HEADS
    width = KEY_VALUE_HEADS * HEAD_SIZE
    factor = math.log2(math.e) / math.sqrt(HEAD_SIZE)
    for kv_head in range(KEY_VALUE_HEADS):
        first = kv_head * HEAD_SIZE
        key_rows = kv_ref[pl.ds(start, window), first : first + HEAD_SIZE]
        value_rows = kv_ref[pl.ds(start, window), width + first : width + first + HEAD_SIZE]
        for pair in range(group // 2):
            at = (kv_head * group + pair * 2) * HEAD_SIZE
            rows = jnp.concatenate(
                [
                    query_ref[:, at : at + HEAD_SIZE],
                    query_ref[:, at + HEAD_SIZE : at + 2 * HEAD_SIZE],
                ],
                axis=0,
            )
            scores = dot_t(rows, key_rows).reshape(2, tokens, window) + bias[None]
            highest = jnp.max(scores, axis=-1, keepdims=True)
            raised = jnp.exp2((scores - highest) * factor)
            total = jnp.sum(raised, axis=-1, keepdims=True)
            mixed = dot(raised.astype(BF16).reshape(2 * tokens, window), value_rows)
            mixed = (mixed.reshape(2, tokens, HEAD_SIZE) / total).astype(BF16)
            out_ref[:, at : at + HEAD_SIZE] = mixed[0]
            out_ref[:, at + HEAD_SIZE : at + 2 * HEAD_SIZE] = mixed[1]


def attend(queries, kv_all, documents, earlier):
    tokens = queries.shape[0]
    length = kv_all.shape[0]
    place = lax.axis_index("seq")
    window = min(length, length // 2 + tokens)
    first_block = jnp.clip(place + 1 - window // tokens, 0, (length - window) // tokens)
    mine = place * tokens + jnp.arange(tokens)
    there = first_block * tokens + jnp.arange(window)
    doc_mine = lax.dynamic_slice_in_dim(documents, place * tokens, tokens)
    doc_there = lax.dynamic_slice_in_dim(documents, first_block * tokens, window)
    allowed = (there[None, :] <= mine[:, None]) & (doc_there[None, :] == doc_mine[:, None])
    bias = jnp.where(allowed, 0.0, -jnp.inf).astype(F32)
    return pl.pallas_call(
        attend_kernel,
        out_shape=jax.ShapeDtypeStruct(queries.shape, BF16),
        in_specs=[
            pl.BlockSpec(memory_space=pltpu.SMEM),
            pl.BlockSpec(memory_space=pltpu.VMEM),
            pl.BlockSpec(memory_space=pltpu.VMEM),
            pl.BlockSpec(memory_space=pltpu.VMEM),
        ]
        + [anywhere()] * len(earlier),
        out_specs=pl.BlockSpec(memory_space=pltpu.VMEM),
        compiler_params=params(),
        name="attend",
    )(first_block.reshape(1).astype(jnp.int32), queries, kv_all, bias, *earlier)


def vmem():
    return pl.BlockSpec(memory_space=pltpu.VMEM)


def anywhere():
    return pl.BlockSpec(memory_space=pl.ANY)


def smem():
    return pl.BlockSpec(memory_space=pltpu.SMEM)


def params(mebibytes=56):
    return pltpu.CompilerParams(vmem_limit_bytes=mebibytes << 20)


def cost(flops, bytes_accessed):
    return pl.CostEstimate(flops=flops, bytes_accessed=bytes_accessed, transcendentals=0)


def project_kernel(*refs, blocks, chunks):
    attended, residuals = refs[:blocks], refs[blocks : 2 * blocks]
    own_ref, pair_ref, gain_ref = refs[2 * blocks : 2 * blocks + 3]
    outs = refs[2 * blocks + 3 :]
    cols = own_ref.shape[1]
    tokens = residuals[0].shape[0]
    rows = jnp.concatenate([ref[...] for ref in attended], axis=0)
    square = None
    for side, weight_ref in enumerate((own_ref, pair_ref)):
        at = side * cols
        stream = dot(rows, weight_ref[...])
        stream += jnp.concatenate([ref[:, at : at + cols] for ref in residuals], axis=0).astype(F32)
        scaled = (stream * gain_ref[:, at : at + cols]).astype(BF16)
        for out_ref, (start, size) in zip(outs, chunks):
            out_ref[: blocks * tokens, side * size : (side + 1) * size] = scaled[
                :, start : start + size
            ]
        for lane in range(0, cols, 128):
            piece = stream[:, lane : lane + 128]
            square = piece * piece if square is None else square + piece * piece
    square = jnp.sum(square.T, axis=0, keepdims=True)
    square = jnp.concatenate(
        [square[:, i * tokens : (i + 1) * tokens] for i in range(blocks)], axis=0
    )
    high = square.astype(BF16).astype(F32)
    rest = jnp.zeros((16 - 2 * blocks, tokens), F32)
    outs[0][blocks * tokens :, :] = jnp.zeros((16, outs[0].shape[1]), BF16)
    outs[0][blocks * tokens :, :tokens] = jnp.concatenate(
        [high, square - high, rest], axis=0
    ).astype(BF16)


def project(attended, residuals, own_weight, pair_weight, gain, chunks):
    blocks = len(attended)
    tokens, width = attended[0].shape
    cols = own_weight.shape[1]
    rows = blocks * tokens
    return pl.pallas_call(
        lambda *refs: project_kernel(*refs, blocks=blocks, chunks=chunks),
        in_specs=[vmem()] * (2 * blocks + 3),
        out_specs=[vmem()] * len(chunks),
        out_shape=[
            jax.ShapeDtypeStruct((rows + (0 if number else 16), 2 * size), BF16)
            for number, (_, size) in enumerate(chunks)
        ],
        compiler_params=params(),
        cost_estimate=cost(4 * rows * width * cols, 4 * width * cols),
        name="project",
    )(*attended, *residuals, own_weight, pair_weight, gain.reshape(1, 2 * cols))


def all_hits(slot_ref, capacity):
    groups, near = slot_ref.shape
    places = lax.broadcasted_iota(jnp.int32, (capacity, near), 0)
    return jnp.concatenate(
        [places == slot_ref[group : group + 1, :] for group in range(groups)], axis=0
    )


def pick_kernel(column_ref, slot_ref, *refs, count, width, first):
    blocks = refs[:count]
    out_ref = refs[-2] if first else refs[-1]
    groups, capacity, cols = out_ref.shape
    near = slot_ref.shape[1]
    tokens = near // count
    half = cols // count
    hits = all_hits(slot_ref, capacity)
    if first:
        inverses = []
        for b in range(count):
            total = jnp.zeros((1, tokens), F32)
            for r in range(b % 2, count, 2):
                table = blocks[r][count // 2 * tokens :, :tokens].astype(F32)
                row = (r ^ b) // 2
                total += table[row : row + 1] + table[count // 2 + row : count // 2 + row + 1]
            inverses.append(lax.rsqrt(total / width + norm_eps))
        inverse = jnp.concatenate(inverses, axis=1)
        refs[-1][...] = inverse
    else:
        inverse = refs[count][...]
    factors = jnp.sum(jnp.where(hits, inverse, 0.0), axis=1, keepdims=True)
    rows = []
    for c in range(count):
        pieces = []
        for b in range(count):
            r = (c // 2) * 2 + b % 2
            q = (r ^ b) // 2
            at = 0 if c == r else half
            pieces.append(blocks[r][q * tokens : (q + 1) * tokens, at : at + half])
        rows.append(jnp.concatenate(pieces, axis=0))
    picked = dot(hits.astype(BF16), jnp.concatenate(rows, axis=1))
    picked = (picked * factors).astype(BF16).reshape(groups, capacity, cols)
    for c in range(count):
        at = pl.multiple_of((column_ref[0] ^ c) * half, 128)
        out_ref[:, :, pl.ds(at, half)] = picked[:, :, c * half : (c + 1) * half]


def pick(column, slots, blocks, capacity, width, inverse=None, earlier=()):
    groups, near = slots.shape
    count = len(blocks)
    first = inverse is None
    cols = blocks[0].shape[1] * count // 2
    out_specs = [vmem()]
    out_shape = [jax.ShapeDtypeStruct((groups, capacity, cols), BF16)]
    if first:
        out_specs.append(vmem())
        out_shape.append(jax.ShapeDtypeStruct((1, near), F32))
    more = () if first else (inverse,)
    made = pl.pallas_call(
        lambda *refs: pick_kernel(
            *refs[: 2 + count + len(more)],
            *refs[2 + count + len(more) + len(earlier) :],
            count=count,
            width=width,
            first=first,
        ),
        in_specs=[smem()]
        + [vmem()] * (1 + len(blocks) + len(more))
        + [anywhere()] * len(earlier),
        out_specs=out_specs,
        out_shape=out_shape,
        compiler_params=params(),
        cost_estimate=cost(2 * groups * capacity * near * cols, 2 * groups * capacity * cols),
        name="pick",
    )(column.reshape(1), slots, *blocks, *more, *earlier)
    return made if first else (made[0], inverse)


def joined(refs):
    return jnp.concatenate(
        [jnp.concatenate([ref[...] for ref in part], axis=0) for part in refs], axis=1
    )


def split(refs, parts):
    count = len(refs) // parts
    return [refs[i * count : (i + 1) * count] for i in range(parts)]


def fill_kernel(slot_ref, *refs, parts):
    out_ref = refs[-1]
    hits = all_hits(slot_ref, out_ref.shape[0] // slot_ref.shape[0]).astype(BF16)
    for number, blocks in enumerate(split(refs[:-1], parts)):
        cols = blocks[0].shape[1]
        rows = jnp.concatenate([ref[...] for ref in blocks], axis=0)
        out_ref[:, number * cols : (number + 1) * cols] = dot(hits, rows).astype(BF16)


def fill(slots, upstream, capacity, earlier):
    groups, near = slots.shape
    blocks = [x for part in upstream for x in part]
    rows, cols = groups * capacity, sum(part[0].shape[1] for part in upstream)
    return pl.pallas_call(
        lambda *refs: fill_kernel(*refs[: 1 + len(blocks)], refs[-1], parts=len(upstream)),
        in_specs=[vmem()] * (1 + len(blocks)) + [anywhere()],
        out_specs=vmem(),
        out_shape=jax.ShapeDtypeStruct((rows, cols), BF16),
        compiler_params=params(),
        cost_estimate=cost(2 * rows * near * cols, 2 * rows * cols),
        name="fill",
    )(slots, *blocks, earlier)


def back_kernel(slot_ref, gate_ref, factor_ref, *refs, parts, capacity):
    out_ref = refs[-1]
    rows = joined(split(refs[:-1], parts))
    groups, rank, _ = out_ref.shape
    made = dot_t(factor_ref[...], rows)
    hits = all_hits(slot_ref, capacity).astype(BF16)
    out_ref[...] = jnp.zeros(out_ref.shape, BF16)
    for group in range(groups):
        mine = made[group * rank : (group + 1) * rank] * gate_ref[group : group + 1, :]
        slots = hits[group * capacity : (group + 1) * capacity]
        out_ref[group, :, :capacity] = dot_t(mine.astype(BF16), slots).astype(BF16)


def back_slots_of(slots, gates, factors, upstream, capacity, earlier):
    groups, near = slots.shape
    blocks = [x for part in upstream for x in part]
    rank = factors.shape[0] // groups
    return pl.pallas_call(
        lambda *refs: back_kernel(
            *refs[: 3 + len(blocks)], refs[-1], parts=len(upstream), capacity=capacity
        ),
        in_specs=[vmem()] * (3 + len(blocks)) + [anywhere()],
        out_specs=vmem(),
        out_shape=jax.ShapeDtypeStruct((groups, rank, capacity + -capacity % 128), BF16),
        compiler_params=params(),
        cost_estimate=cost(2 * near * factors.size, 4 * factors.size),
        name="back_low",
    )(slots, gates, factors, *blocks, earlier)


def gradient_kernel(low_ref, weight_ref, back_ref, *refs, parts, rank):
    out_ref = refs[-1]
    groups, capacity, _ = low_ref.shape
    rows = joined(split(refs[:-1], parts))
    width = rows.shape[1]
    low = low_ref[...].reshape(groups * capacity, low_ref.shape[2]).astype(F32).T[:rank]
    low = jnp.concatenate([low] * groups, axis=0)
    group = lax.broadcasted_iota(jnp.int32, low.shape, 0) // rank
    place = lax.broadcasted_iota(jnp.int32, low.shape, 1) - group * capacity
    low = jnp.where((place >= 0) & (place < capacity), low, 0.0).astype(BF16)
    weighted = dot_t(low, weight_ref[...]).astype(BF16)
    made = dot(weighted, rows).astype(BF16)
    out_ref[:, :, :width] = made.reshape(groups, rank, width)
    out_ref[:, :, width:] = back_ref[...]


def gradient_parts(back, at, weights, back_slots, upstream):
    groups, capacity, _ = back.shape
    near = weights.shape[0]
    rank, wide = back_slots.shape[1:]
    blocks = [x for part in upstream for x in part]
    width = sum(part[0].shape[1] for part in upstream)

    def whole(x):
        return pl.BlockSpec(x.shape, lambda i: (0,) * x.ndim)

    return pl.pallas_call(
        lambda *refs: gradient_kernel(*refs, parts=len(upstream), rank=rank),
        grid=(1,),
        in_specs=[
            pl.BlockSpec((groups, capacity, 128), lambda i: (0, 0, at // 128)),
            whole(weights),
            whole(back_slots),
        ]
        + [whole(x) for x in blocks],
        out_specs=pl.BlockSpec((groups, rank, width + wide), lambda i: (0, 0, 0)),
        out_shape=jax.ShapeDtypeStruct((groups, rank, width + wide), BF16),
        compiler_params=params(),
        cost_estimate=cost(2 * near * groups * rank * (width + groups * capacity), 4 * near * width),
        name="gradient",
    )(back, weights, back_slots, *blocks)


def half_kernel(rows_ref, gate_ref, up_ref, *refs):
    out_gate, out_up = refs[-2:]
    rows = rows_ref[...]
    rows = rows.reshape(rows.shape[0] * rows.shape[1], rows.shape[2])
    gate_weight, up_weight = gate_ref[...], up_ref[...]
    shape = (rows.shape[1], gate_weight.shape[2])
    gate, up = dot(rows, gate_weight.reshape(shape)), dot(rows, up_weight.reshape(shape))
    if len(refs) == 4:
        gate, up = gate + refs[0][...], up + refs[1][...]
    out_gate[...] = gate
    out_up[...] = up


def last_kernel(rows_ref, gate_ref, up_ref, gate_in, up_in, factor_ref, out_active, out_low):
    rows = rows_ref[...]
    rows = rows.reshape(rows.shape[0] * rows.shape[1], rows.shape[2])
    gate_weight, up_weight = gate_ref[...], up_ref[...]
    shape = (rows.shape[1], gate_weight.shape[2])
    gate = dot(rows, gate_weight.reshape(shape)) + gate_in[...]
    up = dot(rows, up_weight.reshape(shape)) + up_in[...]
    active = (gate / (1.0 + jnp.exp(-gate)) * up).astype(BF16)
    out_active[...] = active
    out_low[...] = dot(active, factor_ref[...]).astype(BF16)


def hidden_units(rows, at, gate_weight, up_weight, so_far, factor, earlier=()):
    groups, capacity, cols = rows.shape
    blocks, _, units = gate_weight.shape
    together = max(1, groups // 4)
    step = together * capacity
    part = cols // blocks
    weight = pl.BlockSpec((blocks, part, units), lambda i: (0, at // part, 0))
    sums = pl.BlockSpec((step, units), lambda i: (i, 0))
    in_specs = [pl.BlockSpec((together, capacity, cols), lambda i: (i, 0, 0)), weight, weight]
    in_specs += [sums] * len(so_far)
    more = ()
    if factor is None:
        out_specs = [sums, sums]
        out_shape = [jax.ShapeDtypeStruct((groups * capacity, units), F32)] * 2
    else:
        more = (factor,)
        rank = factor.shape[1]
        in_specs.append(pl.BlockSpec(factor.shape, lambda i: (0, 0)))
        out_specs = [sums, pl.BlockSpec((step, rank), lambda i: (i, 0))]
        out_shape = [
            jax.ShapeDtypeStruct((groups * capacity, units), BF16),
            jax.ShapeDtypeStruct((groups * capacity, rank), BF16),
        ]
    count = 3 + len(so_far) + len(more)
    in_specs += [anywhere()] * len(earlier)
    body = half_kernel if factor is None else last_kernel
    return pl.pallas_call(
        lambda *refs: body(*refs[:count], *refs[count + len(earlier) :]),
        grid=(groups // together,),
        in_specs=in_specs,
        out_specs=out_specs,
        out_shape=out_shape,
        compiler_params=params(),
        cost_estimate=cost(
            4 * groups * capacity * cols * units, 4 * cols * units + 16 * groups * capacity * units
        ),
        name="units",
    )(rows, gate_weight, up_weight, *so_far, *more, *earlier)


def down_kernel(active_ref, low_ref, down_ref, up_ref, out_ref, *, cols):
    low = low_ref[...]
    rows = dot(active_ref[...], down_ref[...]) + adapter_scale * dot(low, up_ref[...])
    together, capacity, wide = out_ref.shape
    out_ref[:, :, :cols] = rows.astype(BF16).reshape(together, capacity, cols)
    if wide > cols:
        out_ref[:, :, cols:] = jnp.zeros((together, capacity, wide - cols), BF16)
        out_ref[:, :, cols : cols + low.shape[1]] = low.reshape(together, capacity, low.shape[1])


def down(active, low, groups, at, cols, extra, down_weight, up_factor, earlier=()):
    rows, units = active.shape
    capacity = rows // groups
    rank = low.shape[1]
    together = max(1, groups // 4)
    step = together * capacity
    return pl.pallas_call(
        lambda *refs: down_kernel(*refs[:4], refs[-1], cols=cols),
        grid=(groups // together,),
        in_specs=[
            pl.BlockSpec((step, units), lambda i: (i, 0)),
            pl.BlockSpec((step, rank), lambda i: (i, 0)),
            pl.BlockSpec((units, cols), lambda i: (0, at // cols)),
            pl.BlockSpec((rank, cols), lambda i: (0, at // cols)),
        ]
        + [anywhere()] * len(earlier),
        out_specs=pl.BlockSpec((together, capacity, cols + extra), lambda i: (i, 0, 0)),
        out_shape=jax.ShapeDtypeStruct((groups, capacity, cols + extra), BF16),
        compiler_params=params(),
        cost_estimate=cost(2 * rows * cols * units, 2 * cols * (units + rows)),
        name="down",
    )(active, low, down_weight, up_factor, *earlier)


def combine_kernel(back_ref, weight_ref, upstream_ref, *refs, cols, blocks, last, first):
    groups, capacity, _ = back_ref.shape
    back = back_ref[:, :, :cols].reshape(groups * capacity, cols)
    dots = jnp.sum(back.astype(F32) * upstream_ref[...].astype(F32), axis=1, keepdims=True)
    if not first:
        dots += refs[0][...]
    outs = refs[-blocks:] if last else refs[-blocks - 1 : -1]
    total = dot(weight_ref[...], back).astype(BF16)
    near = total.shape[0]
    tokens = near // blocks
    for block in range(blocks):
        outs[block][:, :cols] = total[block * tokens : (block + 1) * tokens]
    if not last:
        refs[-1][...] = dots
        return
    slot_ref = refs[1]
    places = lax.broadcasted_iota(jnp.int32, (capacity, near), 0)
    found = []
    for group in range(groups):
        mine = dots[group * capacity : (group + 1) * capacity]
        hits = places == slot_ref[group : group + 1, :]
        found.append(jnp.sum(jnp.where(hits, mine, 0.0), axis=0, keepdims=True))
    found = jnp.concatenate(found, axis=0)
    high = found.astype(BF16).astype(F32)
    rest = jnp.zeros((128 - 2 * groups, near), F32)
    table = jnp.concatenate([high, found - high, rest], axis=0).T.astype(BF16)
    for block in range(blocks):
        outs[block][:, cols:] = table[block * tokens : (block + 1) * tokens]


def combine(back, at, cols, weights, upstream, dots, slots, blocks, last, earlier):
    groups, capacity, wide = back.shape
    near = weights.shape[0]
    tokens = near // blocks
    out_shape = [jax.ShapeDtypeStruct((tokens, cols + (128 if last else 0)), BF16)] * blocks
    if not last:
        out_shape.append(jax.ShapeDtypeStruct((groups * capacity, 1), F32))

    def whole(shape):
        return pl.BlockSpec(shape, lambda i: (0,) * len(shape))

    first = dots is None
    more = () if first else ((dots, slots) if last else (dots,))
    return pl.pallas_call(
        lambda *refs: combine_kernel(
            *refs[: 3 + len(more)],
            *refs[3 + len(more) + len(earlier) :],
            cols=cols,
            blocks=blocks,
            last=last,
            first=first,
        ),
        grid=(1,),
        in_specs=[
            whole(back.shape),
            whole(weights.shape),
            pl.BlockSpec((groups * capacity, cols), lambda i: (0, at // cols)),
        ]
        + [whole(x.shape) for x in more]
        + [anywhere()] * len(earlier),
        out_specs=[whole(s.shape) for s in out_shape],
        out_shape=out_shape,
        compiler_params=params(),
        cost_estimate=cost(
            2 * groups * capacity * near * cols, 2 * cols * (groups * capacity + near)
        ),
        name="combine",
    )(back, weights, upstream, *more, *earlier)


def exchange(xs, axis):
    size = lax.axis_size(axis)
    return [xs[0]] + [
        lax.ppermute(xs[r], axis, [(i, i ^ r) for i in range(size)]) for r in range(1, size)
    ]


def across(x, axis):
    return exchange([x] * lax.axis_size(axis), axis)


def from_plane(x, r):
    size = lax.axis_size("expert")
    return lax.ppermute(x, "expert", [(i, i ^ r) for i in range(size)])


def columns_of(x, r, size):
    return lax.dynamic_slice_in_dim(x, (lax.axis_index("expert") ^ r) * size, size, 1)


def swap(x):
    return lax.all_to_all(x, "seq", split_axis=0, concat_axis=0, tiled=True)


def spread(x):
    count = lax.axis_size("seq")
    return swap(jnp.broadcast_to(x[None], (count,) + x.shape)).reshape(-1, x.shape[-1])


def after(x, *earlier):
    return pl.pallas_call(
        lambda *refs: None,
        in_specs=[anywhere()] * (1 + len(earlier)),
        out_specs=anywhere(),
        out_shape=jax.ShapeDtypeStruct(x.shape, x.dtype),
        input_output_aliases={0: 0},
        name="after",
    )(x, *earlier)


def finish_kernel(*refs, sizes, blocks, groups):
    parts = len(sizes) * blocks
    pieces = refs[:parts]
    probs_ref, ids_ref, names_ref, out_ref, grad_ref = refs[parts:]
    at = 0
    for number, size in enumerate(sizes):
        mine = pieces[number * blocks : (number + 1) * blocks]
        total = mine[0][:, :size].astype(F32)
        for ref in mine[1:]:
            total += ref[:, :size].astype(F32)
        out_ref[:, at : at + size] = total.astype(BF16)
        at += size
    dots = []
    for ref in pieces[-blocks:]:
        table = ref[:, sizes[-1] :].astype(F32)
        dots.append(table[:, :groups] + table[:, groups : 2 * groups])
    dots = jnp.concatenate(dots, axis=1)
    probs, ids, names = probs_ref[...], ids_ref[...], names_ref[...]
    picked = [
        jnp.sum(jnp.where(ids[:, k : k + 1] == names, dots, 0.0), axis=1, keepdims=True)
        for k in range(ids.shape[1])
    ]
    picked = jnp.concatenate(picked, axis=1)
    grad = probs * (picked - jnp.sum(probs * picked, axis=1, keepdims=True))
    rest = jnp.zeros((grad.shape[0], 128 - grad.shape[1]), F32)
    grad_ref[...] = jnp.concatenate([grad, rest], axis=1).T[: grad.shape[1]]


def finish(home, sizes, probs, ids, names, groups):
    tokens = probs.shape[0]
    blocks = len(home[0])
    return pl.pallas_call(
        lambda *refs: finish_kernel(*refs, sizes=sizes, blocks=blocks, groups=groups),
        in_specs=[vmem()] * (blocks * len(sizes) + 3),
        out_specs=[vmem()] * 2,
        out_shape=[
            jax.ShapeDtypeStruct((tokens, sum(sizes)), BF16),
            jax.ShapeDtypeStruct(probs.shape[::-1], F32),
        ],
        compiler_params=params(),
        name="finish",
    )(*[x for pieces in home for x in pieces], probs, ids, names)


def shards(
    queries,
    keys,
    values,
    document_index,
    residual,
    output_projection,
    norm_gain_weight,
    routed_experts,
    router_logits,
    gate_weight,
    up_weight,
    down_weight,
    adapter_down,
    adapter_up,
    cotangent,
):
    seq_devices = lax.axis_size("seq")
    columns = lax.axis_size("expert")
    column = lax.axis_index("expert")
    place = lax.axis_index("seq")
    tokens = queries.shape[1]
    width = queries.shape[2]
    experts = seq_devices * columns
    rank = adapter_up.shape[1]
    near = columns * tokens
    block = width // columns

    kv_own = jnp.concatenate([keys[0], values[0]], axis=1)
    kv_all = spread(kv_own)
    share = output_projection.shape[0] // seq_devices
    pair_share = after(
        lax.dynamic_slice_in_dim(output_projection, place * share, share, 0), kv_own
    )
    pair_share = from_plane(pair_share, 1)
    router_logits = after(router_logits, kv_own)
    gate_probs = jax.nn.softmax(router_logits[0], axis=-1)
    routing = across(
        jnp.concatenate([gate_probs, routed_experts[0].astype(F32)], axis=1),
        "expert",
    )
    residuals = [
        jnp.concatenate([columns_of(residual[0], r, block), columns_of(residual[0], r + 1, block)], 1)
        for r in range(0, columns, 2)
    ]
    residuals = [residuals[0]] + [
        from_plane(after(residuals[r // 2], kv_own), r) for r in range(2, columns, 2)
    ]
    pair_projection = spread(after(pair_share, *residuals[1:], *routing[1:]))
    up_factors = spread(after(adapter_up[0], pair_projection))

    attended = attend(queries[0], kv_all, document_index[0], ())
    attended = [attended] + [from_plane(attended, r) for r in range(2, columns, 2)]

    capacity = columns * (9 * tokens * PICKS_PER_TOKEN // (8 * experts))
    capacity = -(-capacity // 16) * 16
    routing = jnp.concatenate(routing, axis=0)
    near_probs = routing[:, :PICKS_PER_TOKEN]
    near_picks = routing[:, PICKS_PER_TOKEN:].astype(jnp.int32)
    plane_experts = jnp.arange(seq_devices) * columns + column
    hits = near_picks[:, :, None] == plane_experts[None, None, :]
    member = jnp.any(hits, axis=1)
    gates = jnp.sum(jnp.where(hits, near_probs[:, :, None], 0.0), axis=1)
    inner = jnp.arange(near)
    lower = (inner[None, :] < inner[:, None]).astype(BF16)
    ranks = dot(lower, member.astype(BF16)).astype(jnp.int32)
    slot_rows = jnp.where(member, ranks, capacity)
    slots = slot_rows.T
    numbers = jnp.arange(seq_devices * capacity)
    named = jnp.where(member, ranks + jnp.arange(seq_devices)[None, :] * capacity, -1)
    weights = jnp.sum(
        jnp.where(named[:, None, :] == numbers[None, :, None], gates[:, None, :], 0.0), axis=2
    ).astype(BF16)

    chunks = [(0, block // 2), (block // 2, block // 2)]
    gain = norm_gain_weight[None]
    scaled = project(
        attended,
        residuals,
        output_projection,
        pair_projection,
        jnp.concatenate([columns_of(gain, 0, block), columns_of(gain, 1, block)], 1),
        chunks,
    )
    rows, crossed = [], []
    inverse = None
    for number, piece in enumerate(scaled):
        blocks = across(piece, "expert")
        crossed.append(blocks)
        earlier = (up_factors, weights) if number == 0 else ()
        picked, inverse = pick(column, slots, blocks, capacity, width, inverse, earlier)
        rows.append(swap(picked))
    half = width // 2
    upstream = [across(after(cotangent[0, :, :half], *crossed[-1][1:]), "expert")]
    so_far = ()
    for number, (at, cols) in enumerate(chunks):
        last = number == len(chunks) - 1
        so_far = hidden_units(
            rows[number],
            at,
            gate_weight[0].reshape(columns, block, -1),
            up_weight[0].reshape(columns, block, -1),
            so_far,
            adapter_down[0] if last else None,
            tuple(upstream[0][1:]) if last else (),
        )
    active, low_rank = so_far
    upstream.append(across(after(cotangent[0, :, half:], *upstream[0][1:]), "expert"))

    chunks = ((0, half), (half, half))
    adapters = (down_weight[0], adapter_up[0])
    outputs = [down(active, low_rank, seq_devices, 0, half, 128, *adapters)]
    upstream_slots = fill(slots, upstream, capacity, outputs[0])
    back_slots = back_slots_of(slots, gates.T, up_factors, upstream, capacity, outputs[0])
    dots, home, backs = None, [], []
    for number, (at, cols) in enumerate(chunks):
        if number > 0:
            earlier = (outputs[0],)
            outputs.append(down(active, low_rank, seq_devices, at, cols, 0, *adapters, earlier))
        backs.append(swap(after(outputs[number], upstream_slots) if number else outputs[0]))
        last = number == len(chunks) - 1
        *sums, more = combine(
            backs[-1],
            at,
            cols,
            weights,
            upstream_slots,
            dots,
            slots,
            columns,
            last,
            home[-1][1:] if home else [weights],
        )
        if last:
            sums.append(more)
        else:
            dots = more
        home.append(exchange(sums, "expert"))

    parts = gradient_parts(backs[0], half, weights, back_slots, upstream)
    parts = swap(after(parts, home[-1][0]))
    up_factor_gradient = adapter_scale * jnp.sum(parts[:, :, :width].astype(F32), axis=0)
    down_factor_gradient = adapter_scale * jnp.einsum(
        "jcf,jrc->fr",
        active.reshape(seq_devices, capacity, -1),
        parts[:, :, width : width + capacity],
        preferred_element_type=F32,
    )

    names = (
        jnp.arange(seq_devices)[None, :] * columns
        + (column ^ jnp.arange(columns, dtype=jnp.int32))[:, None]
    )
    combined_output, router_logit_gradient = finish(
        home,
        [cols for _, cols in chunks],
        gate_probs,
        routed_experts[0],
        names.reshape(1, experts),
        seq_devices,
    )
    return (
        combined_output[None],
        down_factor_gradient[None],
        up_factor_gradient[None],
        router_logit_gradient.T[None],
    )


def solution(mesh):
    return jax.shard_map(
        shards,
        mesh=mesh,
        in_specs=(
            P(("groups", "expert"), "seq", None),
            P(("groups", "expert"), "seq", None),
            P(("groups", "expert"), "seq", None),
            P(("groups", "expert"), None),
            P(("groups", "expert"), "seq", None),
            P(None, "expert"),
            P(),
            P(("groups", "expert"), "seq", None),
            P(("groups", "expert"), "seq", None),
            P(("seq", "expert"), None, None),
            P(("seq", "expert"), None, None),
            P(("seq", "expert"), None, None),
            P(("seq", "expert"), None, None),
            P(("seq", "expert"), None, None),
            P(("groups", "expert"), "seq", None),
        ),
        out_specs=(
            P(("groups", "expert"), "seq", None),
            P(("groups", "seq", "expert"), None, None),
            P(("groups", "seq", "expert"), None, None),
            P(("groups", "expert"), "seq", None),
        ),
        check_vma=False,
    )
```

```python
import math

import jax
import jax.numpy as jnp
from jax import lax
from jax.experimental import pallas as pl
from jax.experimental.pallas import tpu as pltpu
from jax.sharding import PartitionSpec as P

QUERY_HEADS = 16
KEY_VALUE_HEADS = 2
HEAD_SIZE = 128
PICKS_PER_TOKEN = 8

adapter_scale = 2.0
norm_eps = 1e-06
BF16 = jnp.bfloat16
F32 = jnp.float32


def dot(a, b):
    return jnp.dot(a, b, preferred_element_type=F32)


def dot_t(a, b):
    return lax.dot_general(a, b, (((1,), (1,)), ((), ())), preferred_element_type=F32)


def attend_kernel(start_ref, query_ref, kv_ref, bias_ref, *refs):
    out_ref = refs[-1]
    tokens = query_ref.shape[0]
    window = bias_ref.shape[1]
    start = pl.multiple_of(start_ref[0] * tokens, tokens)
    bias = bias_ref[...]
    group = QUERY_HEADS // KEY_VALUE_HEADS
    width = KEY_VALUE_HEADS * HEAD_SIZE
    factor = math.log2(math.e) / math.sqrt(HEAD_SIZE)
    for kv_head in range(KEY_VALUE_HEADS):
        first = kv_head * HEAD_SIZE
        key_rows = kv_ref[pl.ds(start, window), first : first + HEAD_SIZE]
        value_rows = kv_ref[pl.ds(start, window), width + first : width + first + HEAD_SIZE]
        for pair in range(group // 2):
            at = (kv_head * group + pair * 2) * HEAD_SIZE
            rows = jnp.concatenate(
                [
                    query_ref[:, at : at + HEAD_SIZE],
                    query_ref[:, at + HEAD_SIZE : at + 2 * HEAD_SIZE],
                ],
                axis=0,
            )
            scores = dot_t(rows, key_rows).reshape(2, tokens, window) + bias[None]
            highest = jnp.max(scores, axis=-1, keepdims=True)
            raised = jnp.exp2((scores - highest) * factor)
            total = jnp.sum(raised, axis=-1, keepdims=True)
            mixed = dot(raised.astype(BF16).reshape(2 * tokens, window), value_rows)
            mixed = (mixed.reshape(2, tokens, HEAD_SIZE) / total).astype(BF16)
            out_ref[:, at : at + HEAD_SIZE] = mixed[0]
            out_ref[:, at + HEAD_SIZE : at + 2 * HEAD_SIZE] = mixed[1]


def attend(queries, kv_all, documents, earlier):
    tokens = queries.shape[0]
    length = kv_all.shape[0]
    place = lax.axis_index("seq")
    window = min(length, length // 2 + tokens)
    first_block = jnp.clip(place + 1 - window // tokens, 0, (length - window) // tokens)
    mine = place * tokens + jnp.arange(tokens)
    there = first_block * tokens + jnp.arange(window)
    doc_mine = lax.dynamic_slice_in_dim(documents, place * tokens, tokens)
    doc_there = lax.dynamic_slice_in_dim(documents, first_block * tokens, window)
    allowed = (there[None, :] <= mine[:, None]) & (doc_there[None, :] == doc_mine[:, None])
    bias = jnp.where(allowed, 0.0, -jnp.inf).astype(F32)
    return pl.pallas_call(
        attend_kernel,
        out_shape=jax.ShapeDtypeStruct(queries.shape, BF16),
        in_specs=[
            pl.BlockSpec(memory_space=pltpu.SMEM),
            pl.BlockSpec(memory_space=pltpu.VMEM),
            pl.BlockSpec(memory_space=pltpu.VMEM),
            pl.BlockSpec(memory_space=pltpu.VMEM),
        ]
        + [anywhere()] * len(earlier),
        out_specs=pl.BlockSpec(memory_space=pltpu.VMEM),
        compiler_params=params(),
        name="attend",
    )(first_block.reshape(1).astype(jnp.int32), queries, kv_all, bias, *earlier)


def vmem():
    return pl.BlockSpec(memory_space=pltpu.VMEM)


def anywhere():
    return pl.BlockSpec(memory_space=pl.ANY)


def smem():
    return pl.BlockSpec(memory_space=pltpu.SMEM)


def params(mebibytes=24):
    return pltpu.CompilerParams(vmem_limit_bytes=mebibytes << 20)


def cost(flops, bytes_accessed):
    return pl.CostEstimate(flops=flops, bytes_accessed=bytes_accessed, transcendentals=0)


def project_kernel(*refs, blocks, chunks):
    attended, residuals = refs[:blocks], refs[blocks : 2 * blocks]
    own_ref, pair_ref, gain_ref, routing_ref = refs[2 * blocks : 2 * blocks + 4]
    outs = refs[2 * blocks + 4 :]
    cols = own_ref.shape[1]
    tokens = residuals[0].shape[0]
    rows = jnp.concatenate([ref[...] for ref in attended], axis=0)
    square = None
    for side, weight_ref in enumerate((own_ref, pair_ref)):
        at = side * cols
        stream = dot(rows, weight_ref[...])
        stream += jnp.concatenate([ref[:, at : at + cols] for ref in residuals], axis=0).astype(F32)
        scaled = (stream * gain_ref[:, at : at + cols]).astype(BF16)
        for out_ref, (start, size) in zip(outs, chunks):
            out_ref[: blocks * tokens, side * size : (side + 1) * size] = scaled[
                :, start : start + size
            ]
        for lane in range(0, cols, 128):
            piece = stream[:, lane : lane + 128]
            square = piece * piece if square is None else square + piece * piece
    square = jnp.sum(square.T, axis=0, keepdims=True)
    square = jnp.concatenate(
        [square[:, i * tokens : (i + 1) * tokens] for i in range(blocks)], axis=0
    )
    high = square.astype(BF16).astype(F32)
    routing = routing_ref[...]
    picks = routing.shape[0] // 2
    gates = routing[:picks].astype(BF16).astype(F32)
    rest = outs[0].shape[0] - blocks * tokens - 3 * picks - 2 * blocks
    rest = [jnp.zeros((rest, tokens), F32)] if rest else []
    outs[0][blocks * tokens :, tokens:] = jnp.zeros(
        (outs[0].shape[0] - blocks * tokens, outs[0].shape[1] - tokens), BF16
    )
    outs[0][blocks * tokens :, :tokens] = jnp.concatenate(
        [gates, routing[:picks] - gates, routing[picks:], high, square - high, *rest], axis=0
    ).astype(BF16)


def project(attended, residuals, own_weight, pair_weight, gain, routing, chunks):
    blocks = len(attended)
    tokens, width = attended[0].shape
    cols = own_weight.shape[1]
    rows = blocks * tokens
    more = 3 * routing.shape[0] // 2 + 2 * blocks
    more = -(-more // 16) * 16
    return pl.pallas_call(
        lambda *refs: project_kernel(*refs, blocks=blocks, chunks=chunks),
        in_specs=[vmem()] * (2 * blocks + 4),
        out_specs=[vmem()] * len(chunks),
        out_shape=[
            jax.ShapeDtypeStruct((rows + (0 if number else more), 2 * size), BF16)
            for number, (_, size) in enumerate(chunks)
        ],
        compiler_params=params(),
        cost_estimate=cost(4 * rows * width * cols, 4 * width * cols),
        name="project",
    )(*attended, *residuals, own_weight, pair_weight, gain.reshape(1, 2 * cols), routing)


def hits_of(slots, capacity):
    groups, near = slots.shape
    places = lax.broadcasted_iota(jnp.int32, (capacity, near), 0)
    return jnp.concatenate(
        [
            jnp.where(places == slots[group : group + 1, :], 1.0, 0.0).astype(F32)
            for group in range(groups)
        ],
        axis=0,
    )


def route_kernel(column_ref, *refs, capacity, picks, columns, width):
    blocks = refs[:-4]
    slot_ref, gate_ref, weight_ref, inverse_ref = refs[-4:]
    groups, near = slot_ref.shape
    count = len(blocks)
    tokens = near // count
    tables = [block[near:, :tokens].astype(F32) for block in blocks]
    table = jnp.concatenate(tables, axis=1)
    probs = table[:picks] + table[picks : 2 * picks]
    ids = table[2 * picks : 3 * picks].astype(jnp.int32)
    member, gates = [], []
    for group in range(groups):
        hit = ids == group * columns + column_ref[0]
        member.append(jnp.sum(hit.astype(F32), axis=0, keepdims=True))
        gates.append(jnp.sum(jnp.where(hit, probs, 0.0), axis=0, keepdims=True))
    member = jnp.concatenate(member, axis=0)
    earlier = lax.broadcasted_iota(jnp.int32, (near, near), 0) < lax.broadcasted_iota(
        jnp.int32, (near, near), 1
    )
    ranks = dot(member.astype(BF16), earlier.astype(BF16)).astype(jnp.int32)
    slots = jnp.where(member > 0.0, ranks, capacity)
    slot_ref[...] = slots
    gate_ref[...] = jnp.concatenate(gates, axis=0)
    places = lax.broadcasted_iota(jnp.int32, (capacity, near), 0)
    weights = [
        jnp.where(places == slots[group : group + 1], gates[group], 0.0) for group in range(groups)
    ]
    rows = groups * capacity
    if rows % 128:
        weights.append(jnp.zeros((-rows % 128, near), F32))
    weight_ref[...] = jnp.concatenate(weights, axis=0).T[:, :rows].astype(BF16)
    inverses = []
    for b in range(count):
        total = jnp.zeros((1, tokens), F32)
        for i in range(count):
            row = 3 * picks + (i ^ b)
            total += tables[i][row : row + 1]
            total += tables[i][count + row : count + row + 1]
        inverses.append(lax.rsqrt(total / width + norm_eps))
    inverse_ref[...] = jnp.concatenate(inverses, axis=1)


def route(column, blocks, groups, capacity, tokens, picks, columns, width):
    near = len(blocks) * tokens
    return pl.pallas_call(
        lambda *refs: route_kernel(
            *refs, capacity=capacity, picks=picks, columns=columns, width=width
        ),
        in_specs=[smem()] + [vmem()] * len(blocks),
        out_specs=[vmem()] * 4,
        out_shape=[
            jax.ShapeDtypeStruct((groups, near), jnp.int32),
            jax.ShapeDtypeStruct((groups, near), F32),
            jax.ShapeDtypeStruct((near, groups * capacity), BF16),
            jax.ShapeDtypeStruct((1, near), F32),
        ],
        compiler_params=params(),
        name="route",
    )(column.reshape(1), *blocks)


def pick_kernel(first_ref, slot_ref, inverse_ref, *refs, count, capacity):
    blocks = refs[:count]
    out_ref = refs[-1]
    near = slot_ref.shape[1]
    tokens = near // count
    half = blocks[0].shape[1] // 2
    hits = hits_of(slot_ref[...], capacity)
    factors = jnp.sum(hits * inverse_ref[...], axis=1, keepdims=True)
    hits = hits.astype(BF16)
    for i, block in enumerate(blocks):
        rows = jnp.concatenate(
            [block[(i ^ b) * tokens : ((i ^ b) + 1) * tokens, :] for b in range(count)], axis=0
        )
        picked = (dot(hits, rows) * factors).astype(BF16)
        for side in range(2):
            at = pl.multiple_of((first_ref[0] ^ (2 * i + side)) * half, 128)
            out_ref[:, pl.ds(at, half)] = picked[:, side * half : (side + 1) * half]


def pick(first, slots, inverse, blocks, capacity, earlier):
    groups, near = slots.shape
    count = len(blocks)
    cols = blocks[0].shape[1] * count
    rows = groups * capacity
    return pl.pallas_call(
        lambda *refs: pick_kernel(*refs[: 3 + count], refs[-1], count=count, capacity=capacity),
        in_specs=[smem()] + [vmem()] * (2 + count) + [anywhere()] * len(earlier),
        out_specs=vmem(),
        out_shape=jax.ShapeDtypeStruct((rows, cols), BF16),
        compiler_params=params(),
        cost_estimate=cost(2 * rows * near * cols, 2 * rows * cols),
        name="pick",
    )(first.reshape(1), slots, inverse, *blocks, *earlier)


def fill_kernel(slot_ref, *refs, capacity):
    blocks, out_ref = refs[:-1], refs[-1]
    rows = jnp.concatenate([block[...] for block in blocks], axis=0)
    out_ref[...] = dot(hits_of(slot_ref[...], capacity).astype(BF16), rows).astype(BF16)


def fill(slots, blocks, capacity, earlier):
    groups, near = slots.shape
    rows, cols = groups * capacity, blocks[0].shape[1]
    return pl.pallas_call(
        lambda *refs: fill_kernel(*refs[: 1 + len(blocks)], refs[-1], capacity=capacity),
        in_specs=[vmem()] * (1 + len(blocks)) + [anywhere()],
        out_specs=vmem(),
        out_shape=jax.ShapeDtypeStruct((rows, cols), BF16),
        compiler_params=params(),
        cost_estimate=cost(2 * rows * near * cols, 2 * rows * cols),
        name="fill",
    )(slots, *blocks, earlier)


def back_kernel(factor_ref, *refs, capacity, count):
    out_ref = refs[-1]
    groups, rank, wide = out_ref.shape
    halves = 2
    part = wide // halves
    out_ref[...] = jnp.zeros(out_ref.shape, BF16)
    for half in range(halves):
        slot_ref, gate_ref, *blocks = refs[half * (2 + count) : (half + 1) * (2 + count)]
        rows = jnp.concatenate([block[...] for block in blocks], axis=0)
        made = dot_t(factor_ref[...], rows)
        hits = hits_of(slot_ref[...], capacity)
        for group in range(groups):
            mine = made[group * rank : (group + 1) * rank] * gate_ref[group : group + 1, :]
            slots = hits[group * capacity : (group + 1) * capacity].astype(BF16)
            out_ref[group, :, half * part : half * part + capacity] = dot_t(
                mine.astype(BF16), slots
            ).astype(BF16)


def back_slots_of(factors, halves, capacity, earlier):
    operands = [x for slots, gates, blocks in halves for x in (slots, gates, *blocks)]
    count = len(halves[0][2])
    groups, near = halves[0][0].shape
    rank = factors.shape[0] // groups
    part = capacity + -capacity % 128
    return pl.pallas_call(
        lambda *refs: back_kernel(
            *refs[: 1 + len(operands)], refs[-1], capacity=capacity, count=count
        ),
        in_specs=[vmem()] * (1 + len(operands)) + [anywhere()],
        out_specs=vmem(),
        out_shape=jax.ShapeDtypeStruct((groups, rank, 2 * part), BF16),
        compiler_params=params(),
        cost_estimate=cost(4 * near * factors.size, 4 * factors.size),
        name="back_low",
    )(factors, *operands, earlier)


def gradient_kernel(back_ref, *refs, count, rank):
    out_ref = refs[-1]
    groups = back_ref.shape[0]
    made = 0.0
    for half in range(2):
        low_ref, weight_ref, *blocks = refs[half * (2 + count) : (half + 1) * (2 + count)]
        rows = jnp.concatenate([block[...] for block in blocks], axis=0)
        low = low_ref[...].astype(F32)
        slots = low.shape[0]
        if slots % 128:
            low = jnp.concatenate([low, jnp.zeros((-slots % 128, low.shape[1]), F32)], axis=0)
        low = low.T[:rank, :slots]
        low = jnp.concatenate([low] * groups, axis=0)
        capacity = slots // groups
        group = lax.broadcasted_iota(jnp.int32, low.shape, 0) // rank
        place = lax.broadcasted_iota(jnp.int32, low.shape, 1) - group * capacity
        low = jnp.where((place >= 0) & (place < capacity), low, 0.0).astype(BF16)
        made += dot(dot_t(low, weight_ref[...]).astype(BF16), rows)
    width = made.shape[1]
    out_ref[:, :, :width] = made.astype(BF16).reshape(groups, rank, width)
    out_ref[:, :, width:] = back_ref[...]


def gradient_parts(back_slots, halves, earlier):
    groups, rank, wide = back_slots.shape
    width = halves[0][2][0].shape[1]
    count = len(halves[0][2])
    near = halves[0][1].shape[0]
    operands, in_specs = [back_slots], [pl.BlockSpec(back_slots.shape, lambda i: (0, 0, 0))]
    for back, weights, blocks in halves:
        operands += [back, weights, *blocks]
        in_specs.append(pl.BlockSpec((back.shape[0], 128), lambda i: (0, width // 128)))
        in_specs += [pl.BlockSpec(x.shape, lambda i: (0, 0)) for x in (weights, *blocks)]
    return pl.pallas_call(
        lambda *refs: gradient_kernel(*refs[: len(operands)], refs[-1], count=count, rank=rank),
        grid=(1,),
        in_specs=in_specs + [anywhere()],
        out_specs=pl.BlockSpec((groups, rank, width + wide), lambda i: (0, 0, 0)),
        out_shape=jax.ShapeDtypeStruct((groups, rank, width + wide), BF16),
        compiler_params=params(),
        cost_estimate=cost(4 * near * groups * rank * width, 4 * near * width),
        name="gradient",
    )(*operands, earlier)


def expert_kernel(
    rows_ref, gate_ref, up_ref, factor_ref, down_ref, up_factor_ref, out_active, out_ref
):
    rows = rows_ref[...]
    gate = dot(rows, gate_ref[...])
    up = dot(rows, up_ref[...])
    active = (gate / (1.0 + jnp.exp(-gate)) * up).astype(BF16)
    out_active[...] = active
    low = dot(active, factor_ref[...]).astype(BF16)
    made = dot(active, down_ref[...]) + adapter_scale * dot(low, up_factor_ref[...])
    cols, rank = made.shape[1], low.shape[1]
    out_ref[:, :cols] = made.astype(BF16)
    out_ref[:, cols:] = jnp.zeros((rows.shape[0], out_ref.shape[1] - cols), BF16)
    out_ref[:, cols : cols + rank] = low


def expert(rows, gate_weight, up_weight, factor, down_weight, up_factor, earlier):
    count, width = rows.shape
    units = gate_weight.shape[1]
    step = count // 2

    def whole(x):
        return pl.BlockSpec(x.shape, lambda i: (0, 0))

    weights = (gate_weight, up_weight, factor, down_weight, up_factor)
    return pl.pallas_call(
        lambda *refs: expert_kernel(*refs[:6], *refs[-2:]),
        grid=(count // step,),
        in_specs=[pl.BlockSpec((step, width), lambda i: (i, 0))]
        + [whole(x) for x in weights]
        + [anywhere()] * len(earlier),
        out_specs=[
            pl.BlockSpec((step, units), lambda i: (i, 0)),
            pl.BlockSpec((step, width + 128), lambda i: (i, 0)),
        ],
        out_shape=[
            jax.ShapeDtypeStruct((count, units), BF16),
            jax.ShapeDtypeStruct((count, width + 128), BF16),
        ],
        compiler_params=params(56),
        cost_estimate=cost(0, 0),
        name="expert",
    )(rows, *weights, *earlier)


def combine_kernel(back_ref, weight_ref, upstream_ref, slot_ref, *outs):
    blocks = len(outs)
    cols = upstream_ref.shape[1]
    groups, near = slot_ref.shape
    tokens = near // blocks
    back = back_ref[:, :cols]
    dots = jnp.sum(back.astype(F32) * upstream_ref[...].astype(F32), axis=1, keepdims=True)
    total = dot(weight_ref[...], back).astype(BF16)
    capacity = back.shape[0] // groups
    places = lax.broadcasted_iota(jnp.int32, (capacity, near), 0)
    found = []
    for group in range(groups):
        mine = dots[group * capacity : (group + 1) * capacity]
        hits = places == slot_ref[group : group + 1, :]
        found.append(jnp.sum(jnp.where(hits, mine, 0.0), axis=0, keepdims=True))
    found = jnp.concatenate(found, axis=0)
    high = found.astype(BF16).astype(F32)
    rest = jnp.zeros((128 - 2 * groups, near), F32)
    table = jnp.concatenate([high, found - high, rest], axis=0).T.astype(BF16)
    for block in range(blocks):
        outs[block][:, :cols] = total[block * tokens : (block + 1) * tokens]
        outs[block][:, cols:] = table[block * tokens : (block + 1) * tokens]


def combine(back, weights, upstream, slots, blocks, earlier):
    rows, cols = upstream.shape
    near = weights.shape[0]
    return pl.pallas_call(
        lambda *refs: combine_kernel(*refs[:4], *refs[4 + len(earlier) :]),
        in_specs=[vmem()] * 4 + [anywhere()] * len(earlier),
        out_specs=[vmem()] * blocks,
        out_shape=[jax.ShapeDtypeStruct((near // blocks, cols + 128), BF16)] * blocks,
        compiler_params=params(56),
        cost_estimate=cost(2 * rows * near * cols, 2 * cols * (rows + near)),
        name="combine",
    )(back, weights, upstream, slots, *earlier)


def from_plane(x, r):
    size = lax.axis_size("expert")
    return lax.ppermute(x, "expert", [(i, i ^ r) for i in range(size)])


def columns_of(x, r, size):
    return lax.dynamic_slice_in_dim(x, (lax.axis_index("expert") ^ r) * size, size, 1)


def swap(x):
    return lax.all_to_all(x, "seq", split_axis=0, concat_axis=0, tiled=True)


def spread(x):
    count = lax.axis_size("seq")
    return swap(jnp.broadcast_to(x[None], (count,) + x.shape)).reshape(-1, x.shape[-1])


def after(x, *earlier):
    return pl.pallas_call(
        lambda *refs: None,
        in_specs=[anywhere()] * (1 + len(earlier)),
        out_specs=anywhere(),
        out_shape=jax.ShapeDtypeStruct(x.shape, x.dtype),
        input_output_aliases={0: 0},
        name="after",
    )(x, *earlier)


def sum_kernel(parts_ref, *refs):
    actives, up_ref, down_ref = refs[:-2], refs[-2], refs[-1]
    groups, _, wide = parts_ref.shape
    width = up_ref.shape[1]
    part = (wide - width) // len(actives)
    up = jnp.zeros(up_ref.shape, F32)
    for group in range(groups):
        up += parts_ref[group, :, :width].astype(F32)
    up_ref[...] = adapter_scale * up
    low = jnp.zeros(down_ref.shape, F32)
    for half, active_ref in enumerate(actives):
        capacity = active_ref.shape[0] // groups
        active = active_ref[...].astype(F32)
        at = width + half * part
        for group in range(groups):
            low += dot(
                parts_ref[group, :, at : at + part][:, :capacity],
                active[group * capacity : (group + 1) * capacity].astype(BF16),
            )
    down_ref[...] = adapter_scale * low


def adapter_gradients(parts, actives, width):
    rank = parts.shape[1]
    return pl.pallas_call(
        sum_kernel,
        in_specs=[vmem()] * (1 + len(actives)),
        out_specs=[vmem()] * 2,
        out_shape=[
            jax.ShapeDtypeStruct((rank, width), F32),
            jax.ShapeDtypeStruct((rank, actives[0].shape[1]), F32),
        ],
        compiler_params=params(),
        name="gradients",
    )(parts, *actives)


def finish_kernel(*refs, groups):
    pieces = refs[:-5]
    probs_ref, ids_ref, names_ref, out_ref, grad_ref = refs[-5:]
    cols = out_ref.shape[1]
    total = pieces[0][:, :cols].astype(F32)
    for ref in pieces[1:]:
        total += ref[:, :cols].astype(F32)
    out_ref[...] = total.astype(BF16)
    dots = []
    for ref in pieces:
        table = ref[:, cols:].astype(F32)
        dots.append(table[:, :groups] + table[:, groups : 2 * groups])
    dots = jnp.concatenate(dots, axis=1)
    probs, ids, names = probs_ref[...], ids_ref[...], names_ref[...]
    picked = [
        jnp.sum(jnp.where(ids[:, k : k + 1] == names, dots, 0.0), axis=1, keepdims=True)
        for k in range(ids.shape[1])
    ]
    picked = jnp.concatenate(picked, axis=1)
    grad = probs * (picked - jnp.sum(probs * picked, axis=1, keepdims=True))
    rest = jnp.zeros((grad.shape[0], 128 - grad.shape[1]), F32)
    grad_ref[...] = jnp.concatenate([grad, rest], axis=1).T[: grad.shape[1]]


def finish(pieces, probs, ids, names, groups, earlier):
    tokens = probs.shape[0]
    count = len(pieces) + 3
    return pl.pallas_call(
        lambda *refs: finish_kernel(*refs[:count], *refs[-2:], groups=groups),
        in_specs=[vmem()] * count + [anywhere()],
        out_specs=[vmem()] * 2,
        out_shape=[
            jax.ShapeDtypeStruct((tokens, pieces[0].shape[1] - 128), BF16),
            jax.ShapeDtypeStruct(probs.shape[::-1], F32),
        ],
        compiler_params=params(56),
        name="finish",
    )(*pieces, probs, ids, names, earlier)


def shards(
    queries,
    keys,
    values,
    document_index,
    residual,
    output_projection,
    norm_gain_weight,
    routed_experts,
    router_logits,
    gate_weight,
    up_weight,
    down_weight,
    adapter_down,
    adapter_up,
    cotangent,
):
    seq_devices = lax.axis_size("seq")
    columns = lax.axis_size("expert")
    column = lax.axis_index("expert")
    place = lax.axis_index("seq")
    tokens = queries.shape[1]
    width = queries.shape[2]
    experts = seq_devices * columns
    rank = adapter_up.shape[1]
    near = columns * tokens
    block = width // columns

    kv_own = jnp.concatenate([keys[0], values[0]], axis=1)
    kv_all = spread(kv_own)
    share = output_projection.shape[0] // seq_devices
    pair_share = after(
        lax.dynamic_slice_in_dim(output_projection, place * share, share, 0), kv_own
    )
    pair_share = from_plane(pair_share, 1)
    gate_probs = jax.nn.softmax(router_logits[0].T, axis=0)
    routing = jnp.concatenate([gate_probs, routed_experts[0].T.astype(F32)], axis=0)
    gate_probs = gate_probs.T
    residuals = [
        jnp.concatenate([columns_of(residual[0], r, block), columns_of(residual[0], r + 1, block)], 1)
        for r in range(0, columns, 2)
    ]
    residuals = [residuals[0]] + [
        from_plane(after(residuals[r // 2], kv_own), r) for r in range(2, columns, 2)
    ]
    attended = attend(queries[0], kv_all, document_index[0], ())
    pair_share = jnp.broadcast_to(pair_share[None], (seq_devices,) + pair_share.shape)
    pair_projection = swap(after(pair_share, attended, *residuals[1:]))
    pair_projection = pair_projection.reshape(-1, block)
    attended = [attended] + [from_plane(attended, r) for r in range(2, columns, 2)]

    gain = norm_gain_weight[None]
    scaled = project(
        attended,
        residuals,
        output_projection,
        pair_projection,
        jnp.concatenate([columns_of(gain, 0, block), columns_of(gain, 1, block)], 1),
        routing,
        [(0, block)],
    )[0]
    capacity = columns // 2 * (9 * tokens * PICKS_PER_TOKEN // (8 * experts))
    up_factors = jnp.broadcast_to(adapter_up[0][None], (seq_devices, rank, width))
    up_factors = swap(after(up_factors, scaled)).reshape(-1, width)
    even = range(2, columns, 2)
    odd = range(1, columns, 2)
    crossed = {0: scaled, **{r: from_plane(scaled, r) for r in even}}
    later = after(scaled, *(crossed[r] for r in even))
    crossed.update({r: from_plane(later, r) for r in odd})
    upstream = {0: cotangent[0]}
    later = after(cotangent[0], *(crossed[r] for r in odd))
    upstream.update({r: from_plane(later, r) for r in even})
    later = after(cotangent[0], *(upstream[r] for r in even))
    upstream.update({r: from_plane(later, r) for r in odd})

    halves = []
    for half in range(2):
        blocks = [crossed[r] for r in range(half, columns, 2)]
        slots, gates, weights, inverse = route(
            column, blocks, seq_devices, capacity, tokens, PICKS_PER_TOKEN, columns, width
        )
        earlier = (up_factors,) if half == 0 else ()
        rows = swap(pick(column ^ half, slots, inverse, blocks, capacity, earlier))
        cotangents = [upstream[r] for r in range(half, columns, 2)]
        halves.append((slots, gates, weights, rows, cotangents))
    made = [
        expert(
            rows,
            gate_weight[0],
            up_weight[0],
            adapter_down[0],
            down_weight[0],
            adapter_up[0],
            (),
        )
        for half, (_, _, _, rows, cotangents) in enumerate(halves)
    ]

    filled = [
        fill(slots, cotangents, capacity, made[1][0]) for slots, _, _, _, cotangents in halves
    ]
    backs, pieces, earlier = [], {}, ()
    for half, (slots, _, weights, _, _) in enumerate(halves):
        sent = after(made[half][1], *(filled if half else [upstream[r] for r in even]))
        backs.append(swap(sent))
        sums = combine(backs[half], weights, filled[half], slots, columns // 2, earlier)
        planes = range(half, columns, 2)
        pieces.update({r: from_plane(x, r) if r else x for r, x in zip(planes, sums)})
        earlier = tuple(pieces[r] for r in planes if r)

    back_slots = back_slots_of(
        up_factors,
        [(slots, gates, cotangents) for slots, gates, _, _, cotangents in halves],
        capacity,
        pieces[0],
    )
    parts = gradient_parts(
        back_slots,
        [(back, half[2], half[4]) for back, half in zip(backs, halves)],
        sums[0],
    )
    up_factor_gradient, down_factor_gradient = adapter_gradients(
        swap(parts), [x[0] for x in made], width
    )

    names = (
        jnp.arange(seq_devices)[None, :] * columns
        + (column ^ jnp.arange(columns, dtype=jnp.int32))[:, None]
    )
    combined_output, router_logit_gradient = finish(
        [pieces[r] for r in range(columns)],
        gate_probs,
        routed_experts[0],
        names.reshape(1, experts),
        seq_devices,
        pieces[0],
    )
    return (
        combined_output[None],
        down_factor_gradient.T[None],
        up_factor_gradient[None],
        router_logit_gradient.T[None],
    )


def solution(mesh):
    return jax.shard_map(
        shards,
        mesh=mesh,
        in_specs=(
            P(("groups", "expert"), "seq", None),
            P(("groups", "expert"), "seq", None),
            P(("groups", "expert"), "seq", None),
            P(("groups", "expert"), None),
            P(("groups", "expert"), "seq", None),
            P(None, "expert"),
            P(),
            P(("groups", "expert"), "seq", None),
            P(("groups", "expert"), "seq", None),
            P(("seq", "expert"), None, None),
            P(("seq", "expert"), None, None),
            P(("seq", "expert"), None, None),
            P(("seq", "expert"), None, None),
            P(("seq", "expert"), None, None),
            P(("groups", "expert"), "seq", None),
        ),
        out_specs=(
            P(("groups", "expert"), "seq", None),
            P(("groups", "seq", "expert"), None, None),
            P(("groups", "seq", "expert"), None, None),
            P(("groups", "expert"), "seq", None),
        ),
        check_vma=False,
    )
```

```python
import math

import jax
import jax.numpy as jnp
from jax import lax
from jax.experimental import pallas as pl
from jax.experimental.pallas import tpu as pltpu
from jax.sharding import PartitionSpec as P

QUERY_HEADS = 16
KEY_VALUE_HEADS = 2
HEAD_SIZE = 128
PICKS_PER_TOKEN = 8

adapter_scale = 2.0
norm_eps = 1e-06
BF16 = jnp.bfloat16
F32 = jnp.float32


def dot(a, b):
    return jnp.dot(a, b, preferred_element_type=F32)


def dot_t(a, b):
    return lax.dot_general(a, b, (((1,), (1,)), ((), ())), preferred_element_type=F32)


def attend_kernel(start_ref, query_ref, kv_ref, bias_ref, *refs):
    out_ref = refs[-1]
    tokens = query_ref.shape[0]
    window = bias_ref.shape[1]
    start = pl.multiple_of(start_ref[0] * tokens, tokens)
    bias = bias_ref[...]
    group = QUERY_HEADS // KEY_VALUE_HEADS
    width = KEY_VALUE_HEADS * HEAD_SIZE
    factor = math.log2(math.e) / math.sqrt(HEAD_SIZE)
    for kv_head in range(KEY_VALUE_HEADS):
        first = kv_head * HEAD_SIZE
        key_rows = kv_ref[pl.ds(start, window), first : first + HEAD_SIZE]
        value_rows = kv_ref[pl.ds(start, window), width + first : width + first + HEAD_SIZE]
        for pair in range(group // 2):
            at = (kv_head * group + pair * 2) * HEAD_SIZE
            rows = jnp.concatenate(
                [
                    query_ref[:, at : at + HEAD_SIZE],
                    query_ref[:, at + HEAD_SIZE : at + 2 * HEAD_SIZE],
                ],
                axis=0,
            )
            scores = dot_t(rows, key_rows).reshape(2, tokens, window) + bias[None]
            highest = jnp.max(scores, axis=-1, keepdims=True)
            raised = jnp.exp2((scores - highest) * factor)
            total = jnp.sum(raised, axis=-1, keepdims=True)
            mixed = dot(raised.astype(BF16).reshape(2 * tokens, window), value_rows)
            mixed = (mixed.reshape(2, tokens, HEAD_SIZE) / total).astype(BF16)
            out_ref[:, at : at + HEAD_SIZE] = mixed[0]
            out_ref[:, at + HEAD_SIZE : at + 2 * HEAD_SIZE] = mixed[1]


def attend(queries, kv_all, documents, earlier):
    tokens = queries.shape[0]
    length = kv_all.shape[0]
    place = lax.axis_index("seq")
    window = min(length, length // 2 + tokens)
    first_block = jnp.clip(place + 1 - window // tokens, 0, (length - window) // tokens)
    mine = place * tokens + jnp.arange(tokens)
    there = first_block * tokens + jnp.arange(window)
    doc_mine = lax.dynamic_slice_in_dim(documents, place * tokens, tokens)
    doc_there = lax.dynamic_slice_in_dim(documents, first_block * tokens, window)
    allowed = (there[None, :] <= mine[:, None]) & (doc_there[None, :] == doc_mine[:, None])
    bias = jnp.where(allowed, 0.0, -jnp.inf).astype(F32)
    return pl.pallas_call(
        attend_kernel,
        out_shape=jax.ShapeDtypeStruct(queries.shape, BF16),
        in_specs=[
            pl.BlockSpec(memory_space=pltpu.SMEM),
            pl.BlockSpec(memory_space=pltpu.VMEM),
            pl.BlockSpec(memory_space=pltpu.VMEM),
            pl.BlockSpec(memory_space=pltpu.VMEM),
        ]
        + [anywhere()] * len(earlier),
        out_specs=pl.BlockSpec(memory_space=pltpu.VMEM),
        compiler_params=params(),
        name="attend",
    )(first_block.reshape(1).astype(jnp.int32), queries, kv_all, bias, *earlier)


def vmem():
    return pl.BlockSpec(memory_space=pltpu.VMEM)


def anywhere():
    return pl.BlockSpec(memory_space=pl.ANY)


def smem():
    return pl.BlockSpec(memory_space=pltpu.SMEM)


def params(mebibytes=24):
    return pltpu.CompilerParams(vmem_limit_bytes=mebibytes << 20)


def cost(flops, bytes_accessed):
    return pl.CostEstimate(flops=flops, bytes_accessed=bytes_accessed, transcendentals=0)


def project_kernel(*refs, blocks, chunks):
    attended, residuals = refs[:blocks], refs[blocks : 2 * blocks]
    own_ref, pair_ref, gain_ref, routing_ref = refs[2 * blocks : 2 * blocks + 4]
    outs = refs[2 * blocks + 4 :]
    cols = own_ref.shape[1]
    tokens = residuals[0].shape[0]
    rows = jnp.concatenate([ref[...] for ref in attended], axis=0)
    square = None
    for side, weight_ref in enumerate((own_ref, pair_ref)):
        at = side * cols
        stream = dot(rows, weight_ref[...])
        stream += jnp.concatenate([ref[:, at : at + cols] for ref in residuals], axis=0).astype(F32)
        scaled = (stream * gain_ref[:, at : at + cols]).astype(BF16)
        for out_ref, (start, size) in zip(outs, chunks):
            out_ref[: blocks * tokens, side * size : (side + 1) * size] = scaled[
                :, start : start + size
            ]
        for lane in range(0, cols, 128):
            piece = stream[:, lane : lane + 128]
            square = piece * piece if square is None else square + piece * piece
    square = jnp.sum(square.T, axis=0, keepdims=True)
    square = jnp.concatenate(
        [square[:, i * tokens : (i + 1) * tokens] for i in range(blocks)], axis=0
    )
    high = square.astype(BF16).astype(F32)
    routing = routing_ref[...]
    picks = routing.shape[0] // 2
    gates = routing[:picks].astype(BF16).astype(F32)
    rest = jnp.zeros((8 - blocks, tokens), F32)
    table = jnp.concatenate(
        [
            jnp.concatenate([gates, routing[:picks] - gates], axis=0),
            jnp.concatenate([routing[picks:], jnp.zeros((picks, tokens), F32)], axis=0),
            jnp.concatenate([high, rest, square - high, rest], axis=0),
        ],
        axis=1,
    )
    wide = table.shape[1]
    out_ref = outs[0]
    out_ref[blocks * tokens :, :wide] = table.astype(BF16)
    if wide < out_ref.shape[1]:
        out_ref[blocks * tokens :, wide:] = jnp.zeros((16, out_ref.shape[1] - wide), BF16)


def project(attended, residuals, own_weight, pair_weight, gain, routing, chunks):
    blocks = len(attended)
    tokens, width = attended[0].shape
    cols = own_weight.shape[1]
    rows = blocks * tokens
    more = 16
    return pl.pallas_call(
        lambda *refs: project_kernel(*refs, blocks=blocks, chunks=chunks),
        in_specs=[vmem()] * (2 * blocks + 4),
        out_specs=[vmem()] * len(chunks),
        out_shape=[
            jax.ShapeDtypeStruct((rows + (0 if number else more), 2 * size), BF16)
            for number, (_, size) in enumerate(chunks)
        ],
        compiler_params=params(),
        cost_estimate=cost(4 * rows * width * cols, 4 * width * cols),
        name="project",
    )(*attended, *residuals, own_weight, pair_weight, gain.reshape(1, 2 * cols), routing)


def hits_of(slots, capacity):
    groups, near = slots.shape
    places = lax.broadcasted_iota(jnp.int32, (capacity, near), 0)
    return jnp.concatenate(
        [
            jnp.where(places == slots[group : group + 1, :], 1.0, 0.0).astype(F32)
            for group in range(groups)
        ],
        axis=0,
    )


def route_kernel(column_ref, *refs, capacity, picks, columns, width):
    blocks = refs[:-3]
    slot_ref, gate_ref, inverse_ref = refs[-3:]
    groups, near = slot_ref.shape
    count = len(blocks)
    tokens = near // count
    tables = [block[near:, :].astype(F32) for block in blocks]
    probs = jnp.concatenate([x[:, :tokens] for x in tables], axis=1)
    probs = probs[:picks] + probs[picks : 2 * picks]
    ids = jnp.concatenate([x[:picks, tokens : 2 * tokens] for x in tables], axis=1)
    ids = ids.astype(jnp.int32)
    squares = [x[:, 2 * tokens : 3 * tokens] for x in tables]
    member, gates = [], []
    for group in range(groups):
        hit = ids == group * columns + column_ref[0]
        member.append(jnp.sum(hit.astype(F32), axis=0, keepdims=True))
        gates.append(jnp.sum(jnp.where(hit, probs, 0.0), axis=0, keepdims=True))
    member = jnp.concatenate(member, axis=0)
    earlier = lax.broadcasted_iota(jnp.int32, (near, near), 0) < lax.broadcasted_iota(
        jnp.int32, (near, near), 1
    )
    ranks = dot(member.astype(BF16), earlier.astype(BF16)).astype(jnp.int32)
    slots = jnp.where(member > 0.0, ranks, capacity)
    slot_ref[...] = slots
    gate_ref[...] = jnp.concatenate(gates, axis=0)
    inverses = []
    for b in range(count):
        total = jnp.zeros((1, tokens), F32)
        for i in range(count):
            row = i ^ b
            total += squares[i][row : row + 1] + squares[i][8 + row : 9 + row]
        inverses.append(lax.rsqrt(total / width + norm_eps))
    inverse_ref[...] = jnp.concatenate(inverses, axis=1)


def route(column, blocks, groups, capacity, tokens, picks, columns, width):
    near = len(blocks) * tokens
    return pl.pallas_call(
        lambda *refs: route_kernel(
            *refs, capacity=capacity, picks=picks, columns=columns, width=width
        ),
        in_specs=[smem()] + [vmem()] * len(blocks),
        out_specs=[vmem()] * 3,
        out_shape=[
            jax.ShapeDtypeStruct((groups, near), jnp.int32),
            jax.ShapeDtypeStruct((groups, near), F32),
            jax.ShapeDtypeStruct((1, near), F32),
        ],
        compiler_params=params(),
        name="route",
    )(column.reshape(1), *blocks)


def pick_kernel(first_ref, slot_ref, inverse_ref, *refs, count, capacity):
    blocks = refs[:count]
    out_ref = refs[-1]
    near = slot_ref.shape[1]
    tokens = near // count
    half = blocks[0].shape[1] // 2
    hits = hits_of(slot_ref[...], capacity)
    factors = jnp.sum(hits * inverse_ref[...], axis=1, keepdims=True)
    hits = hits.astype(BF16)
    for i, block in enumerate(blocks):
        rows = jnp.concatenate(
            [block[(i ^ b) * tokens : ((i ^ b) + 1) * tokens, :] for b in range(count)], axis=0
        )
        picked = (dot(hits, rows) * factors).astype(BF16)
        for side in range(2):
            at = pl.multiple_of((first_ref[0] ^ (2 * i + side)) * half, 128)
            out_ref[:, pl.ds(at, half)] = picked[:, side * half : (side + 1) * half]


def pick(first, slots, inverse, blocks, capacity, earlier):
    groups, near = slots.shape
    count = len(blocks)
    cols = blocks[0].shape[1] * count
    rows = groups * capacity
    return pl.pallas_call(
        lambda *refs: pick_kernel(*refs[: 3 + count], refs[-1], count=count, capacity=capacity),
        in_specs=[smem()] + [vmem()] * (2 + count) + [anywhere()] * len(earlier),
        out_specs=vmem(),
        out_shape=jax.ShapeDtypeStruct((rows, cols), BF16),
        compiler_params=params(),
        cost_estimate=cost(2 * rows * near * cols, 2 * rows * cols),
        name="pick",
    )(first.reshape(1), slots, inverse, *blocks, *earlier)


def fill_kernel(slot_ref, gate_ref, *refs, capacity):
    blocks, out_ref, weight_ref = refs[:-2], refs[-2], refs[-1]
    rows = jnp.concatenate([block[...] for block in blocks], axis=0)
    hits = hits_of(slot_ref[...], capacity)
    out_ref[...] = dot(hits.astype(BF16), rows).astype(BF16)
    count, near = hits.shape
    gates = [
        hits[group * capacity : (group + 1) * capacity] * gate_ref[group : group + 1, :]
        for group in range(gate_ref.shape[0])
    ]
    if count % 128:
        gates.append(jnp.zeros((-count % 128, near), F32))
    weight_ref[...] = jnp.concatenate(gates, axis=0).T[:, :count].astype(BF16)


def fill(slots, gates, blocks, capacity, earlier):
    groups, near = slots.shape
    rows, cols = groups * capacity, blocks[0].shape[1]
    return pl.pallas_call(
        lambda *refs: fill_kernel(*refs[: 2 + len(blocks)], *refs[-2:], capacity=capacity),
        in_specs=[vmem()] * (2 + len(blocks)) + [anywhere()],
        out_specs=[vmem()] * 2,
        out_shape=[
            jax.ShapeDtypeStruct((rows, cols), BF16),
            jax.ShapeDtypeStruct((near, rows), BF16),
        ],
        compiler_params=params(),
        cost_estimate=cost(2 * rows * near * cols, 2 * rows * cols),
        name="fill",
    )(slots, gates, *blocks, earlier)


def back_kernel(factor_ref, *refs, capacity, count):
    out_ref = refs[-1]
    groups, rank, wide = out_ref.shape
    halves = 2
    part = wide // halves
    out_ref[...] = jnp.zeros(out_ref.shape, BF16)
    for half in range(halves):
        slot_ref, gate_ref, *blocks = refs[half * (2 + count) : (half + 1) * (2 + count)]
        rows = jnp.concatenate([block[...] for block in blocks], axis=0)
        made = dot_t(factor_ref[...], rows)
        hits = hits_of(slot_ref[...], capacity)
        for group in range(groups):
            mine = made[group * rank : (group + 1) * rank] * gate_ref[group : group + 1, :]
            slots = hits[group * capacity : (group + 1) * capacity].astype(BF16)
            out_ref[group, :, half * part : half * part + capacity] = dot_t(
                mine.astype(BF16), slots
            ).astype(BF16)


def back_slots_of(factors, halves, capacity, earlier):
    operands = [x for slots, gates, blocks in halves for x in (slots, gates, *blocks)]
    count = len(halves[0][2])
    groups, near = halves[0][0].shape
    rank = factors.shape[0] // groups
    part = capacity + -capacity % 128
    return pl.pallas_call(
        lambda *refs: back_kernel(
            *refs[: 1 + len(operands)], refs[-1], capacity=capacity, count=count
        ),
        in_specs=[vmem()] * (1 + len(operands)) + [anywhere()],
        out_specs=vmem(),
        out_shape=jax.ShapeDtypeStruct((groups, rank, 2 * part), BF16),
        compiler_params=params(),
        cost_estimate=cost(4 * near * factors.size, 4 * factors.size),
        name="back_low",
    )(factors, *operands, earlier)


def gradient_kernel(back_ref, *refs, count, rank):
    out_ref = refs[-1]
    groups = back_ref.shape[0]
    made = 0.0
    for half in range(2):
        low_ref, weight_ref, *blocks = refs[half * (2 + count) : (half + 1) * (2 + count)]
        rows = jnp.concatenate([block[...] for block in blocks], axis=0)
        low = low_ref[...].astype(F32)
        slots = low.shape[0]
        if slots % 128:
            low = jnp.concatenate([low, jnp.zeros((-slots % 128, low.shape[1]), F32)], axis=0)
        low = low.T[:rank, :slots]
        low = jnp.concatenate([low] * groups, axis=0)
        capacity = slots // groups
        group = lax.broadcasted_iota(jnp.int32, low.shape, 0) // rank
        place = lax.broadcasted_iota(jnp.int32, low.shape, 1) - group * capacity
        low = jnp.where((place >= 0) & (place < capacity), low, 0.0).astype(BF16)
        made += dot(dot_t(low, weight_ref[...]).astype(BF16), rows)
    width = made.shape[1]
    out_ref[:, :, :width] = made.astype(BF16).reshape(groups, rank, width)
    out_ref[:, :, width:] = back_ref[...]


def gradient_parts(back_slots, halves, earlier):
    groups, rank, wide = back_slots.shape
    width = halves[0][2][0].shape[1]
    count = len(halves[0][2])
    near = halves[0][1].shape[0]
    operands, in_specs = [back_slots], [pl.BlockSpec(back_slots.shape, lambda i: (0, 0, 0))]
    for back, weights, blocks in halves:
        operands += [back, weights, *blocks]
        in_specs.append(pl.BlockSpec((back.shape[0], 128), lambda i: (0, width // 128)))
        in_specs += [pl.BlockSpec(x.shape, lambda i: (0, 0)) for x in (weights, *blocks)]
    return pl.pallas_call(
        lambda *refs: gradient_kernel(*refs[: len(operands)], refs[-1], count=count, rank=rank),
        grid=(1,),
        in_specs=in_specs + [anywhere()],
        out_specs=pl.BlockSpec((groups, rank, width + wide), lambda i: (0, 0, 0)),
        out_shape=jax.ShapeDtypeStruct((groups, rank, width + wide), BF16),
        compiler_params=params(),
        cost_estimate=cost(4 * near * groups * rank * width, 4 * near * width),
        name="gradient",
    )(*operands, earlier)


def expert_kernel(
    rows_ref, gate_ref, up_ref, factor_ref, down_ref, up_factor_ref, out_active, out_ref
):
    rows = rows_ref[...]
    gate = dot(rows, gate_ref[...])
    up = dot(rows, up_ref[...])
    active = (gate / (1.0 + jnp.exp(-gate)) * up).astype(BF16)
    out_active[...] = active
    low = dot(active, factor_ref[...]).astype(BF16)
    made = dot(active, down_ref[...]) + adapter_scale * dot(low, up_factor_ref[...])
    cols, rank = made.shape[1], low.shape[1]
    out_ref[:, :cols] = made.astype(BF16)
    out_ref[:, cols:] = jnp.zeros((rows.shape[0], out_ref.shape[1] - cols), BF16)
    out_ref[:, cols : cols + rank] = low


def expert(rows, gate_weight, up_weight, factor, down_weight, up_factor, earlier):
    count, width = rows.shape
    units = gate_weight.shape[1]
    step = count // 2

    def whole(x):
        return pl.BlockSpec(x.shape, lambda i: (0, 0))

    weights = (gate_weight, up_weight, factor, down_weight, up_factor)
    return pl.pallas_call(
        lambda *refs: expert_kernel(*refs[:6], *refs[-2:]),
        grid=(count // step,),
        in_specs=[pl.BlockSpec((step, width), lambda i: (i, 0))]
        + [whole(x) for x in weights]
        + [anywhere()] * len(earlier),
        out_specs=[
            pl.BlockSpec((step, units), lambda i: (i, 0)),
            pl.BlockSpec((step, width + 128), lambda i: (i, 0)),
        ],
        out_shape=[
            jax.ShapeDtypeStruct((count, units), BF16),
            jax.ShapeDtypeStruct((count, width + 128), BF16),
        ],
        compiler_params=params(40),
        cost_estimate=cost(0, 0),
        name="expert",
    )(rows, *weights, *earlier)


def combine_kernel(back_ref, weight_ref, upstream_ref, slot_ref, *outs):
    blocks = len(outs)
    cols = upstream_ref.shape[1]
    groups, near = slot_ref.shape
    tokens = near // blocks
    back = back_ref[:, :cols]
    dots = jnp.sum(back.astype(F32) * upstream_ref[...].astype(F32), axis=1, keepdims=True)
    total = dot(weight_ref[...], back).astype(BF16)
    capacity = back.shape[0] // groups
    places = lax.broadcasted_iota(jnp.int32, (capacity, near), 0)
    found = []
    for group in range(groups):
        mine = dots[group * capacity : (group + 1) * capacity]
        hits = places == slot_ref[group : group + 1, :]
        found.append(jnp.sum(jnp.where(hits, mine, 0.0), axis=0, keepdims=True))
    found = jnp.concatenate(found, axis=0)
    high = found.astype(BF16).astype(F32)
    rest = jnp.zeros((128 - 2 * groups, near), F32)
    table = jnp.concatenate([high, found - high, rest], axis=0).T.astype(BF16)
    for block in range(blocks):
        outs[block][:, :cols] = total[block * tokens : (block + 1) * tokens]
        outs[block][:, cols:] = table[block * tokens : (block + 1) * tokens]


def combine(back, weights, upstream, slots, blocks, earlier):
    rows, cols = upstream.shape
    near = weights.shape[0]
    return pl.pallas_call(
        lambda *refs: combine_kernel(*refs[:4], *refs[4 + len(earlier) :]),
        in_specs=[vmem()] * 4 + [anywhere()] * len(earlier),
        out_specs=[vmem()] * blocks,
        out_shape=[jax.ShapeDtypeStruct((near // blocks, cols + 128), BF16)] * blocks,
        compiler_params=params(40),
        cost_estimate=cost(2 * rows * near * cols, 2 * cols * (rows + near)),
        name="combine",
    )(back, weights, upstream, slots, *earlier)


def from_plane(x, r):
    size = lax.axis_size("expert")
    return lax.ppermute(x, "expert", [(i, i ^ r) for i in range(size)])


def columns_of(x, r, size):
    return lax.dynamic_slice_in_dim(x, (lax.axis_index("expert") ^ r) * size, size, 1)


def swap(x):
    return lax.all_to_all(x, "seq", split_axis=0, concat_axis=0, tiled=True)


def after(x, *earlier):
    return pl.pallas_call(
        lambda *refs: None,
        in_specs=[anywhere()] * (1 + len(earlier)),
        out_specs=anywhere(),
        out_shape=jax.ShapeDtypeStruct(x.shape, x.dtype),
        input_output_aliases={0: 0},
        name="after",
    )(x, *earlier)


def sum_kernel(parts_ref, *refs):
    actives, up_ref, down_ref = refs[:-2], refs[-2], refs[-1]
    groups, _, wide = parts_ref.shape
    width = up_ref.shape[1]
    part = (wide - width) // len(actives)
    up = jnp.zeros(up_ref.shape, F32)
    for group in range(groups):
        up += parts_ref[group, :, :width].astype(F32)
    up_ref[...] = adapter_scale * up
    low = jnp.zeros(down_ref.shape, F32)
    for half, active_ref in enumerate(actives):
        capacity = active_ref.shape[0] // groups
        active = active_ref[...].astype(F32)
        at = width + half * part
        for group in range(groups):
            low += dot(
                parts_ref[group, :, at : at + part][:, :capacity],
                active[group * capacity : (group + 1) * capacity].astype(BF16),
            )
    down_ref[...] = adapter_scale * low


def adapter_gradients(parts, actives, width):
    rank = parts.shape[1]
    return pl.pallas_call(
        sum_kernel,
        in_specs=[vmem()] * (1 + len(actives)),
        out_specs=[vmem()] * 2,
        out_shape=[
            jax.ShapeDtypeStruct((rank, width), F32),
            jax.ShapeDtypeStruct((rank, actives[0].shape[1]), F32),
        ],
        compiler_params=params(),
        name="gradients",
    )(parts, *actives)


def finish_kernel(*refs, groups):
    pieces = refs[:-5]
    probs_ref, ids_ref, names_ref, out_ref, grad_ref = refs[-5:]
    cols = out_ref.shape[1]
    total = pieces[0][:, :cols].astype(F32)
    for ref in pieces[1:]:
        total += ref[:, :cols].astype(F32)
    out_ref[...] = total.astype(BF16)
    dots = []
    for ref in pieces:
        table = ref[:, cols:].astype(F32)
        dots.append(table[:, :groups] + table[:, groups : 2 * groups])
    dots = jnp.concatenate(dots, axis=1)
    probs, ids, names = probs_ref[...], ids_ref[...], names_ref[...]
    picked = [
        jnp.sum(jnp.where(ids[:, k : k + 1] == names, dots, 0.0), axis=1, keepdims=True)
        for k in range(ids.shape[1])
    ]
    picked = jnp.concatenate(picked, axis=1)
    grad = probs * (picked - jnp.sum(probs * picked, axis=1, keepdims=True))
    rest = jnp.zeros((grad.shape[0], 128 - grad.shape[1]), F32)
    grad_ref[...] = jnp.concatenate([grad, rest], axis=1).T[: grad.shape[1]]


def finish(pieces, probs, ids, names, groups, earlier):
    tokens = probs.shape[0]
    count = len(pieces) + 3
    return pl.pallas_call(
        lambda *refs: finish_kernel(*refs[:count], *refs[-2:], groups=groups),
        in_specs=[vmem()] * count + [anywhere()],
        out_specs=[vmem()] * 2,
        out_shape=[
            jax.ShapeDtypeStruct((tokens, pieces[0].shape[1] - 128), BF16),
            jax.ShapeDtypeStruct(probs.shape[::-1], F32),
        ],
        compiler_params=params(40),
        name="finish",
    )(*pieces, probs, ids, names, earlier)


def shards(
    queries,
    keys,
    values,
    document_index,
    residual,
    output_projection,
    norm_gain_weight,
    routed_experts,
    router_logits,
    gate_weight,
    up_weight,
    down_weight,
    adapter_down,
    adapter_up,
    cotangent,
):
    seq_devices = lax.axis_size("seq")
    columns = lax.axis_size("expert")
    column = lax.axis_index("expert")
    place = lax.axis_index("seq")
    tokens = queries.shape[1]
    width = queries.shape[2]
    experts = seq_devices * columns
    rank = adapter_up.shape[1]
    near = columns * tokens
    block = width // columns

    kv_own = jnp.concatenate([keys[0], values[0]], axis=1)
    kv_own = jnp.broadcast_to(kv_own[None], (seq_devices,) + kv_own.shape)
    kv_all = swap(kv_own).reshape(seq_devices * tokens, -1)
    share = output_projection.shape[0] // seq_devices
    pair_share = after(
        lax.dynamic_slice_in_dim(output_projection, place * share, share, 0), kv_own
    )
    pair_share = from_plane(pair_share, 1)
    gate_probs = jax.nn.softmax(router_logits[0].T, axis=0)
    routing = jnp.concatenate([gate_probs, routed_experts[0].T.astype(F32)], axis=0)
    gate_probs = gate_probs.T
    residuals = [
        jnp.concatenate([columns_of(residual[0], r, block), columns_of(residual[0], r + 1, block)], 1)
        for r in range(0, columns, 2)
    ]
    residuals = [residuals[0]] + [
        from_plane(after(residuals[r // 2], kv_own), r) for r in range(2, columns, 2)
    ]
    pair_share = jnp.broadcast_to(pair_share[None], (seq_devices,) + pair_share.shape)
    up_wide = jnp.broadcast_to(adapter_up[0][None], (seq_devices, rank, width))
    attended = attend(queries[0], kv_all, document_index[0], (pair_share, up_wide))
    pair_projection = swap(after(pair_share, attended, *residuals[1:]))
    pair_projection = pair_projection.reshape(-1, block)
    attended = [attended] + [from_plane(attended, r) for r in range(2, columns, 2)]

    gain = norm_gain_weight[None]
    scaled = project(
        attended,
        residuals,
        output_projection,
        pair_projection,
        jnp.concatenate([columns_of(gain, 0, block), columns_of(gain, 1, block)], 1),
        routing,
        [(0, block)],
    )[0]
    capacity = columns // 2 * (9 * tokens * PICKS_PER_TOKEN // (8 * experts))
    up_factors = swap(after(up_wide, scaled)).reshape(-1, width)
    even = range(2, columns, 2)
    odd = range(1, columns, 2)
    crossed = {0: scaled, **{r: from_plane(scaled, r) for r in even}}
    later = after(scaled, *(crossed[r] for r in even))
    crossed.update({r: from_plane(later, r) for r in odd})
    upstream = {0: cotangent[0]}
    later = after(cotangent[0], *(crossed[r] for r in odd))
    upstream.update({r: from_plane(later, r) for r in even})
    later = after(cotangent[0], *(upstream[r] for r in even))
    upstream.update({r: from_plane(later, r) for r in odd})

    halves = []
    for half in range(2):
        blocks = [crossed[r] for r in range(half, columns, 2)]
        slots, gates, inverse = route(
            column, blocks, seq_devices, capacity, tokens, PICKS_PER_TOKEN, columns, width
        )
        earlier = (up_factors,) if half == 0 else ()
        rows = swap(pick(column ^ half, slots, inverse, blocks, capacity, earlier))
        cotangents = [upstream[r] for r in range(half, columns, 2)]
        halves.append((slots, gates, rows, cotangents))
    made = [
        expert(
            rows,
            gate_weight[0],
            up_weight[0],
            adapter_down[0],
            down_weight[0],
            adapter_up[0],
            (),
        )
        for _, _, rows, _ in halves
    ]

    filled = [
        fill(slots, gates, cotangents, capacity, made[1][0])
        for slots, gates, _, cotangents in halves
    ]
    backs, pieces, earlier = [], {}, ()
    for half, (slots, _, _, _) in enumerate(halves):
        earlier_sent = [x[0] for x in filled] if half else [upstream[r] for r in even]
        sent = after(made[half][1], *earlier_sent)
        backs.append(swap(sent))
        rows, weights = filled[half]
        sums = combine(backs[half], weights, rows, slots, columns // 2, earlier)
        planes = range(half, columns, 2)
        pieces.update({r: from_plane(x, r) if r else x for r, x in zip(planes, sums)})
        earlier = tuple(pieces[r] for r in planes if r)

    back_slots = back_slots_of(
        up_factors,
        [(slots, gates, cotangents) for slots, gates, _, cotangents in halves],
        capacity,
        pieces[0],
    )
    parts = gradient_parts(
        back_slots,
        [(back, fills[1], half[3]) for back, fills, half in zip(backs, filled, halves)],
        sums[0],
    )
    up_factor_gradient, down_factor_gradient = adapter_gradients(
        swap(parts), [x[0] for x in made], width
    )

    names = (
        jnp.arange(seq_devices)[None, :] * columns
        + (column ^ jnp.arange(columns, dtype=jnp.int32))[:, None]
    )
    combined_output, router_logit_gradient = finish(
        [pieces[r] for r in range(columns)],
        gate_probs,
        routed_experts[0],
        names.reshape(1, experts),
        seq_devices,
        up_factor_gradient,
    )
    return (
        combined_output[None],
        down_factor_gradient.T[None],
        up_factor_gradient[None],
        router_logit_gradient.T[None],
    )


def solution(mesh):
    return jax.shard_map(
        shards,
        mesh=mesh,
        in_specs=(
            P(("groups", "expert"), "seq", None),
            P(("groups", "expert"), "seq", None),
            P(("groups", "expert"), "seq", None),
            P(("groups", "expert"), None),
            P(("groups", "expert"), "seq", None),
            P(None, "expert"),
            P(),
            P(("groups", "expert"), "seq", None),
            P(("groups", "expert"), "seq", None),
            P(("seq", "expert"), None, None),
            P(("seq", "expert"), None, None),
            P(("seq", "expert"), None, None),
            P(("seq", "expert"), None, None),
            P(("seq", "expert"), None, None),
            P(("groups", "expert"), "seq", None),
        ),
        out_specs=(
            P(("groups", "expert"), "seq", None),
            P(("groups", "seq", "expert"), None, None),
            P(("groups", "seq", "expert"), None, None),
            P(("groups", "expert"), "seq", None),
        ),
        check_vma=False,
    )
```

```python
import math

import jax
import jax.numpy as jnp
from jax import lax
from jax.experimental import pallas as pl
from jax.experimental.pallas import tpu as pltpu
from jax.sharding import PartitionSpec as P

QUERY_HEADS = 16
KEY_VALUE_HEADS = 2
HEAD_SIZE = 128
PICKS_PER_TOKEN = 8

adapter_scale = 2.0
norm_eps = 1e-06
BF16 = jnp.bfloat16
F32 = jnp.float32


def dot(a, b):
    return jnp.dot(a, b, preferred_element_type=F32)


def dot_t(a, b):
    return lax.dot_general(a, b, (((1,), (1,)), ((), ())), preferred_element_type=F32)


def attend_kernel(start_ref, query_ref, kv_ref, bias_ref, *refs):
    out_ref = refs[-1]
    tokens = query_ref.shape[0]
    window = bias_ref.shape[1]
    start = pl.multiple_of(start_ref[0] * tokens, tokens)
    bias = bias_ref[...]
    group = QUERY_HEADS // KEY_VALUE_HEADS
    width = KEY_VALUE_HEADS * HEAD_SIZE
    factor = math.log2(math.e) / math.sqrt(HEAD_SIZE)
    for kv_head in range(KEY_VALUE_HEADS):
        first = kv_head * HEAD_SIZE
        key_rows = kv_ref[pl.ds(start, window), first : first + HEAD_SIZE]
        value_rows = kv_ref[pl.ds(start, window), width + first : width + first + HEAD_SIZE]
        for pair in range(group // 2):
            at = (kv_head * group + pair * 2) * HEAD_SIZE
            rows = jnp.concatenate(
                [
                    query_ref[:, at : at + HEAD_SIZE],
                    query_ref[:, at + HEAD_SIZE : at + 2 * HEAD_SIZE],
                ],
                axis=0,
            )
            scores = dot_t(rows, key_rows).reshape(2, tokens, window) + bias[None]
            highest = jnp.max(scores, axis=-1, keepdims=True)
            raised = jnp.exp2((scores - highest) * factor)
            total = jnp.sum(raised, axis=-1, keepdims=True)
            mixed = dot(raised.astype(BF16).reshape(2 * tokens, window), value_rows)
            mixed = (mixed.reshape(2, tokens, HEAD_SIZE) / total).astype(BF16)
            out_ref[:, at : at + HEAD_SIZE] = mixed[0]
            out_ref[:, at + HEAD_SIZE : at + 2 * HEAD_SIZE] = mixed[1]


def attend(queries, kv_all, documents, earlier):
    tokens = queries.shape[0]
    length = kv_all.shape[0]
    place = lax.axis_index("seq")
    window = min(length, length // 2 + tokens)
    first_block = jnp.clip(place + 1 - window // tokens, 0, (length - window) // tokens)
    mine = place * tokens + jnp.arange(tokens)
    there = first_block * tokens + jnp.arange(window)
    doc_mine = lax.dynamic_slice_in_dim(documents, place * tokens, tokens)
    doc_there = lax.dynamic_slice_in_dim(documents, first_block * tokens, window)
    allowed = (there[None, :] <= mine[:, None]) & (doc_there[None, :] == doc_mine[:, None])
    bias = jnp.where(allowed, 0.0, -jnp.inf).astype(F32)
    return pl.pallas_call(
        attend_kernel,
        out_shape=jax.ShapeDtypeStruct(queries.shape, BF16),
        in_specs=[
            pl.BlockSpec(memory_space=pltpu.SMEM),
            pl.BlockSpec(memory_space=pltpu.VMEM),
            pl.BlockSpec(memory_space=pltpu.VMEM),
            pl.BlockSpec(memory_space=pltpu.VMEM),
        ]
        + [anywhere()] * len(earlier),
        out_specs=pl.BlockSpec(memory_space=pltpu.VMEM),
        compiler_params=params(),
        name="attend",
    )(first_block.reshape(1).astype(jnp.int32), queries, kv_all, bias, *earlier)


def vmem():
    return pl.BlockSpec(memory_space=pltpu.VMEM)


def anywhere():
    return pl.BlockSpec(memory_space=pl.ANY)


def smem():
    return pl.BlockSpec(memory_space=pltpu.SMEM)


def params(mebibytes=24):
    return pltpu.CompilerParams(vmem_limit_bytes=mebibytes << 20)


def cost(flops, bytes_accessed):
    return pl.CostEstimate(flops=flops, bytes_accessed=bytes_accessed, transcendentals=0)


def pack_kernel(residual_ref, routing_ref, out_ref):
    tokens = residual_ref.shape[0]
    out_ref[:tokens, :] = residual_ref[...]
    routing = routing_ref[...]
    picks = routing.shape[0] // 2
    gates = routing[:picks].astype(BF16).astype(F32)
    table = jnp.concatenate(
        [
            jnp.concatenate([gates, routing[:picks] - gates], axis=0),
            jnp.concatenate([routing[picks:], jnp.zeros((picks, tokens), F32)], axis=0),
        ],
        axis=1,
    )
    wide = table.shape[1]
    out_ref[tokens:, :wide] = table.astype(BF16)
    if wide < out_ref.shape[1]:
        out_ref[tokens:, wide:] = jnp.zeros((16, out_ref.shape[1] - wide), BF16)


def pack(residual, routing):
    tokens, cols = residual.shape
    return pl.pallas_call(
        pack_kernel,
        in_specs=[vmem()] * 2,
        out_specs=vmem(),
        out_shape=jax.ShapeDtypeStruct((tokens + 16, cols), BF16),
        compiler_params=params(),
        name="pack",
    )(residual, routing)


def tile_place(number, cols):
    across = cols // 128
    return number // across * 16, number % across * 128


def project_kernel(*refs, blocks):
    attended, residuals = refs[:blocks], refs[blocks : 2 * blocks]
    own_ref, pair_ref, gain_ref, out_ref = refs[2 * blocks :]
    cols = own_ref.shape[1]
    tokens = attended[0].shape[0]
    near = blocks * tokens
    rows = jnp.concatenate([ref[...] for ref in attended], axis=0)
    square = None
    for side, weight_ref in enumerate((own_ref, pair_ref)):
        at = side * cols
        stream = dot(rows, weight_ref[...])
        stream += jnp.concatenate(
            [ref[:tokens, at : at + cols] for ref in residuals], axis=0
        ).astype(F32)
        out_ref[:near, at : at + cols] = (stream * gain_ref[:, at : at + cols]).astype(BF16)
        for lane in range(0, cols, 128):
            piece = stream[:, lane : lane + 128]
            square = piece * piece if square is None else square + piece * piece
    square = jnp.sum(square.T, axis=0, keepdims=True)
    square = jnp.concatenate(
        [square[:, i * tokens : (i + 1) * tokens] for i in range(blocks)], axis=0
    )
    high = square.astype(BF16).astype(F32)
    rest = jnp.zeros((8 - blocks, tokens), F32)
    out_ref[near:, :] = jnp.zeros((out_ref.shape[0] - near, 2 * cols), BF16)
    for i, ref in enumerate(residuals):
        row, lane = tile_place(2 * i, 2 * cols)
        out_ref[near + row : near + row + 16, lane : lane + 2 * tokens] = ref[
            tokens:, : 2 * tokens
        ]
    row, lane = tile_place(2 * blocks, 2 * cols)
    out_ref[near + row : near + row + 16, lane : lane + tokens] = jnp.concatenate(
        [high, rest, square - high, rest], axis=0
    ).astype(BF16)


def project(attended, residuals, own_weight, pair_weight, gain):
    blocks = len(attended)
    tokens, width = attended[0].shape
    cols = own_weight.shape[1]
    rows = blocks * tokens
    more = tile_place(2 * blocks, 2 * cols)[0] + 16
    return pl.pallas_call(
        lambda *refs: project_kernel(*refs, blocks=blocks),
        in_specs=[vmem()] * (2 * blocks + 3),
        out_specs=vmem(),
        out_shape=jax.ShapeDtypeStruct((rows + more, 2 * cols), BF16),
        compiler_params=params(),
        cost_estimate=cost(4 * rows * width * cols, 4 * width * cols),
        name="project",
    )(*attended, *residuals, own_weight, pair_weight, gain.reshape(1, 2 * cols))


def hits_of(slots, capacity):
    groups, near = slots.shape
    places = lax.broadcasted_iota(jnp.int32, (capacity, near), 0)
    return jnp.concatenate(
        [
            jnp.where(places == slots[group : group + 1, :], 1.0, 0.0).astype(F32)
            for group in range(groups)
        ],
        axis=0,
    )


def route_kernel(column_ref, *refs, places, capacity, picks, columns):
    blocks, slot_ref, gate_ref = refs[:-2], refs[-2], refs[-1]
    groups, near = slot_ref.shape
    tokens = near // len(places)
    tables = [
        blocks[number][row : row + 16, lane : lane + 2 * tokens].astype(F32)
        for number, row, lane in places
    ]
    probs = jnp.concatenate([x[:, :tokens] for x in tables], axis=1)
    probs = probs[:picks] + probs[picks : 2 * picks]
    ids = jnp.concatenate([x[:picks, tokens:] for x in tables], axis=1).astype(jnp.int32)
    member, gates = [], []
    for group in range(groups):
        hit = ids == group * columns + column_ref[0]
        member.append(jnp.sum(hit.astype(F32), axis=0, keepdims=True))
        gates.append(jnp.sum(jnp.where(hit, probs, 0.0), axis=0, keepdims=True))
    member = jnp.concatenate(member, axis=0)
    earlier = lax.broadcasted_iota(jnp.int32, (near, near), 0) < lax.broadcasted_iota(
        jnp.int32, (near, near), 1
    )
    ranks = dot(member.astype(BF16), earlier.astype(BF16)).astype(jnp.int32)
    slot_ref[...] = jnp.where(member > 0.0, ranks, capacity)
    gate_ref[...] = jnp.concatenate(gates, axis=0)


def route(column, blocks, places, groups, capacity, tokens, picks, columns):
    near = len(places) * tokens
    return pl.pallas_call(
        lambda *refs: route_kernel(
            *refs, places=places, capacity=capacity, picks=picks, columns=columns
        ),
        in_specs=[smem()] + [vmem()] * len(blocks),
        out_specs=[vmem()] * 2,
        out_shape=[
            jax.ShapeDtypeStruct((groups, near), jnp.int32),
            jax.ShapeDtypeStruct((groups, near), F32),
        ],
        compiler_params=params(),
        name="route",
    )(column.reshape(1), *blocks)


def place_sides(out_ref, picked, at, first):
    half = picked.shape[1] // 2
    for side in range(2):
        lane = pl.multiple_of(at + ((first ^ side) % 2) * half, 128)
        out_ref[:, pl.ds(lane, half)] = picked[:, side * half : (side + 1) * half]


def pick_kernel(first_ref, slot_ref, *refs, count, capacity, first, rest):
    blocks, out_ref = refs[:count], refs[-1]
    near = slot_ref.shape[1]
    hits = hits_of(slot_ref[...], capacity)
    places = hits.astype(BF16)
    cols = blocks[0].shape[1]
    skip = 0 if first else cols
    if first:
        picked = dot(places, blocks[0][:near, :]).astype(BF16)
        place_sides(out_ref, picked, 0, first_ref[0])
    if not rest:
        return
    tokens = near // count
    row, lane = tile_place(2 * count, cols)
    squares = [
        x[near + row : near + row + 16, lane : lane + tokens].astype(F32) for x in blocks
    ]
    inverses = []
    for b in range(count):
        total = jnp.zeros((1, tokens), F32)
        for i in range(count):
            total += squares[i][i ^ b : (i ^ b) + 1] + squares[i][8 + (i ^ b) : 9 + (i ^ b)]
        inverses.append(lax.rsqrt(total / (count * cols) + norm_eps))
    factors = jnp.sum(hits * jnp.concatenate(inverses, axis=1), axis=1, keepdims=True)
    for i in range(1, count):
        rows = jnp.concatenate(
            [blocks[i][(i ^ b) * tokens : ((i ^ b) + 1) * tokens, :] for b in range(count)], axis=0
        )
        place_sides(out_ref, dot(places, rows).astype(BF16), i * cols - skip, first_ref[0])
    high = factors.astype(BF16).astype(F32)
    lanes = lax.broadcasted_iota(jnp.int32, (factors.shape[0], 128), 1)
    table = jnp.where(lanes == 0, high, jnp.where(lanes == 1, factors - high, 0.0))
    out_ref[:, count * cols - skip :] = table.astype(BF16)


def pick(plane, slots, blocks, capacity, first, rest, earlier):
    groups, near = slots.shape
    count = len(blocks)
    rows, cols = groups * capacity, blocks[0].shape[1]
    wide = (cols if first else 0) + ((count - 1) * cols + 128 if rest else 0)
    return pl.pallas_call(
        lambda *refs: pick_kernel(
            *refs[: 2 + count],
            refs[-1],
            count=count,
            capacity=capacity,
            first=first,
            rest=rest,
        ),
        in_specs=[smem()] + [vmem()] * (1 + count) + [anywhere()] * len(earlier),
        out_specs=vmem(),
        out_shape=jax.ShapeDtypeStruct((rows, wide), BF16),
        compiler_params=params(),
        cost_estimate=cost(2 * rows * near * wide, 2 * rows * wide),
        name="pick",
    )(plane.reshape(1), slots, *blocks, *earlier)


def fill_kernel(slot_ref, gate_ref, *refs, capacity):
    blocks, out_ref, weight_ref = refs[:-2], refs[-2], refs[-1]
    rows = jnp.concatenate([block[...] for block in blocks], axis=0)
    hits = hits_of(slot_ref[...], capacity)
    out_ref[...] = dot(hits.astype(BF16), rows).astype(BF16)
    count, near = hits.shape
    gates = [
        hits[group * capacity : (group + 1) * capacity] * gate_ref[group : group + 1, :]
        for group in range(gate_ref.shape[0])
    ]
    if count % 128:
        gates.append(jnp.zeros((-count % 128, near), F32))
    weight_ref[...] = jnp.concatenate(gates, axis=0).T[:, :count].astype(BF16)


def fill(slots, gates, blocks, capacity, earlier):
    groups, near = slots.shape
    rows, cols = groups * capacity, blocks[0].shape[1]
    return pl.pallas_call(
        lambda *refs: fill_kernel(*refs[: 2 + len(blocks)], *refs[-2:], capacity=capacity),
        in_specs=[vmem()] * (2 + len(blocks)) + [anywhere()] * len(earlier),
        out_specs=[vmem()] * 2,
        out_shape=[
            jax.ShapeDtypeStruct((rows, cols), BF16),
            jax.ShapeDtypeStruct((near, rows), BF16),
        ],
        compiler_params=params(),
        cost_estimate=cost(2 * rows * near * cols, 2 * rows * cols),
        name="fill",
    )(slots, gates, *blocks, *earlier)


def back_kernel(place_ref, *refs, capacity, count):
    out_ref, made_ref = refs[-2:]
    groups, rank, wide = out_ref.shape
    factors = jnp.concatenate([ref[...] for ref in refs[:groups]], axis=0)
    refs = refs[groups:]
    halves = 2
    part = wide // halves
    out_ref[...] = jnp.zeros(out_ref.shape, BF16)
    for half in range(halves):
        slot_ref, gate_ref, *blocks = refs[half * (2 + count) : (half + 1) * (2 + count)]
        rows = jnp.concatenate([block[...] for block in blocks], axis=0)
        made_ref[...] = dot_t(factors, rows)
        hits = hits_of(slot_ref[...], capacity)
        for group in range(groups):
            x = place_ref[0] ^ group
            at = pl.multiple_of((x // 2 + x % 2 * (groups // 2)) * rank, rank)
            mine = made_ref[pl.ds(at, rank), :] * gate_ref[group : group + 1, :]
            slots = hits[group * capacity : (group + 1) * capacity].astype(BF16)
            out_ref[group, :, half * part : half * part + capacity] = dot_t(
                mine.astype(BF16), slots
            ).astype(BF16)


def back_slots_of(place, factors, halves, capacity, earlier):
    operands = [x for slots, gates, blocks in halves for x in (slots, gates, *blocks)]
    count = len(halves[0][2])
    groups, near = halves[0][0].shape
    rank, width = factors[0].shape
    part = capacity + -capacity % 128
    return pl.pallas_call(
        lambda *refs: back_kernel(
            *refs[: 1 + groups + len(operands)], *refs[-2:], capacity=capacity, count=count
        ),
        in_specs=[smem()] + [vmem()] * (groups + len(operands)) + [anywhere()],
        out_specs=vmem(),
        out_shape=jax.ShapeDtypeStruct((groups, rank, 2 * part), BF16),
        compiler_params=params(),
        scratch_shapes=[pltpu.VMEM((groups * rank, near), F32)],
        cost_estimate=cost(4 * near * groups * rank * width, 4 * groups * rank * width),
        name="back_low",
    )(place.reshape(1), *factors, *operands, earlier)


def gradient_kernel(back_ref, *refs, count, rank):
    out_ref = refs[-1]
    groups = back_ref.shape[0]
    made = 0.0
    for half in range(2):
        low_ref, weight_ref, *blocks = refs[half * (2 + count) : (half + 1) * (2 + count)]
        rows = jnp.concatenate([block[...] for block in blocks], axis=0)
        low = low_ref[...].astype(F32)
        slots = low.shape[0]
        if slots % 128:
            low = jnp.concatenate([low, jnp.zeros((-slots % 128, low.shape[1]), F32)], axis=0)
        low = low.T[:rank, :slots]
        low = jnp.concatenate([low] * groups, axis=0)
        capacity = slots // groups
        group = lax.broadcasted_iota(jnp.int32, low.shape, 0) // rank
        place = lax.broadcasted_iota(jnp.int32, low.shape, 1) - group * capacity
        low = jnp.where((place >= 0) & (place < capacity), low, 0.0).astype(BF16)
        made += dot(dot_t(low, weight_ref[...]).astype(BF16), rows)
    width = made.shape[1]
    out_ref[:, :, :width] = made.astype(BF16).reshape(groups, rank, width)
    out_ref[:, :, width:] = back_ref[...]


def gradient_parts(back_slots, halves, earlier):
    groups, rank, wide = back_slots.shape
    width = halves[0][2][0].shape[1]
    count = len(halves[0][2])
    near = halves[0][1].shape[0]
    operands, in_specs = [back_slots], [pl.BlockSpec(back_slots.shape, lambda i: (0, 0, 0))]
    for back, weights, blocks in halves:
        operands += [back, weights, *blocks]
        in_specs.append(pl.BlockSpec((back.shape[0], 128), lambda i: (0, width // 128)))
        in_specs += [pl.BlockSpec(x.shape, lambda i: (0, 0)) for x in (weights, *blocks)]
    return pl.pallas_call(
        lambda *refs: gradient_kernel(*refs[: len(operands)], refs[-1], count=count, rank=rank),
        grid=(1,),
        in_specs=in_specs + [anywhere()],
        out_specs=pl.BlockSpec((groups, rank, width + wide), lambda i: (0, 0, 0)),
        out_shape=jax.ShapeDtypeStruct((groups, rank, width + wide), BF16),
        compiler_params=params(),
        cost_estimate=cost(4 * near * groups * rank * width, 4 * near * width),
        name="gradient",
    )(*operands, earlier)


def expert_kernel(
    pair_ref,
    *refs,
    cols,
):
    *parts, gate_ref, up_ref, factor_ref, down_ref, up_factor_ref, out_active, out_ref = refs
    more_ref = parts[-1]
    skip = cols if len(parts) > 1 else 0
    gate = up = 0.0
    for i in range(gate_ref.shape[0] // cols):
        if i == 0:
            rows = parts[0][:, :cols]
        else:
            rows = more_ref[:, i * cols - skip : (i + 1) * cols - skip]
        at = pl.ds(pl.multiple_of((pair_ref[0] ^ i) * cols, cols), cols)
        gate += dot(rows, gate_ref[at, :])
        up += dot(rows, up_ref[at, :])
    norm = more_ref[:, more_ref.shape[1] - 128 :].astype(F32)
    norm = norm[:, :1] + norm[:, 1:2]
    gate, up = gate * norm, up * norm
    active = (gate / (1.0 + jnp.exp(-gate)) * up).astype(BF16)
    out_active[...] = active
    low = dot(active, factor_ref[...]).astype(BF16)
    made = dot(active, down_ref[...]) + adapter_scale * dot(low, up_factor_ref[...])
    cols, rank = made.shape[1], low.shape[1]
    out_ref[:, :cols] = made.astype(BF16)
    out_ref[:, cols:] = jnp.zeros((made.shape[0], out_ref.shape[1] - cols), BF16)
    out_ref[:, cols : cols + rank] = low


def expert(pair, parts, cols, gate_weight, up_weight, factor, down_weight, up_factor):
    count = parts[0].shape[0]
    width, units = gate_weight.shape
    step = count // 2

    def whole(x):
        return pl.BlockSpec(x.shape, lambda i: (0, 0))

    weights = (gate_weight, up_weight, factor, down_weight, up_factor)
    return pl.pallas_call(
        lambda *refs: expert_kernel(*refs, cols=cols),
        grid=(count // step,),
        in_specs=[smem()]
        + [pl.BlockSpec((step, x.shape[1]), lambda i: (i, 0)) for x in parts]
        + [whole(x) for x in weights],
        out_specs=[
            pl.BlockSpec((step, units), lambda i: (i, 0)),
            pl.BlockSpec((step, width + 128), lambda i: (i, 0)),
        ],
        out_shape=[
            jax.ShapeDtypeStruct((count, units), BF16),
            jax.ShapeDtypeStruct((count, width + 128), BF16),
        ],
        compiler_params=params(40),
        cost_estimate=cost(0, 0),
        name="expert",
    )(pair.reshape(1), *parts, *weights)


def combine_kernel(back_ref, weight_ref, upstream_ref, slot_ref, *outs):
    blocks = len(outs)
    cols = upstream_ref.shape[1]
    groups, near = slot_ref.shape
    tokens = near // blocks
    back = back_ref[:, :cols]
    dots = jnp.sum(back.astype(F32) * upstream_ref[...].astype(F32), axis=1, keepdims=True)
    total = dot(weight_ref[...], back).astype(BF16)
    capacity = back.shape[0] // groups
    places = lax.broadcasted_iota(jnp.int32, (capacity, near), 0)
    found = []
    for group in range(groups):
        mine = dots[group * capacity : (group + 1) * capacity]
        hits = places == slot_ref[group : group + 1, :]
        found.append(jnp.sum(jnp.where(hits, mine, 0.0), axis=0, keepdims=True))
    found = jnp.concatenate(found, axis=0)
    high = found.astype(BF16).astype(F32)
    rest = jnp.zeros((128 - 2 * groups, near), F32)
    table = jnp.concatenate([high, found - high, rest], axis=0).T.astype(BF16)
    for block in range(blocks):
        outs[block][:, :cols] = total[block * tokens : (block + 1) * tokens]
        outs[block][:, cols:] = table[block * tokens : (block + 1) * tokens]


def combine(back, weights, upstream, slots, blocks, earlier):
    rows, cols = upstream.shape
    near = weights.shape[0]
    return pl.pallas_call(
        lambda *refs: combine_kernel(*refs[:4], *refs[4 + len(earlier) :]),
        in_specs=[vmem()] * 4 + [anywhere()] * len(earlier),
        out_specs=[vmem()] * blocks,
        out_shape=[jax.ShapeDtypeStruct((near // blocks, cols + 128), BF16)] * blocks,
        compiler_params=params(40),
        cost_estimate=cost(2 * rows * near * cols, 2 * cols * (rows + near)),
        name="combine",
    )(back, weights, upstream, slots, *earlier)


def from_plane(x, r):
    size = lax.axis_size("expert")
    return lax.ppermute(x, "expert", [(i, i ^ r) for i in range(size)])


def from_place(x, r):
    size = lax.axis_size("seq")
    return lax.ppermute(x, "seq", [(i, i ^ r) for i in range(size)])


def copy_kernel(x_ref, *refs):
    refs[-1][...] = x_ref[...]


def later(x, *earlier):
    return pl.pallas_call(
        copy_kernel,
        in_specs=[vmem()] + [anywhere()] * len(earlier),
        out_specs=vmem(),
        out_shape=jax.ShapeDtypeStruct(x.shape, x.dtype),
        compiler_params=params(),
        name="later",
    )(x, *earlier)


def all_planes(x):
    found = [x, from_plane(x, 1)]
    for r in range(2, lax.axis_size("expert"), 2):
        found.append(from_plane(x, r))
        found.append(from_plane(found[-1], 1))
    return found


def columns_of(x, r, size):
    return lax.dynamic_slice_in_dim(x, (lax.axis_index("expert") ^ r) * size, size, 1)


def swap(x):
    return lax.all_to_all(x, "seq", split_axis=0, concat_axis=0, tiled=True)


def after(x, *earlier):
    return pl.pallas_call(
        lambda *refs: None,
        in_specs=[anywhere()] * (1 + len(earlier)),
        out_specs=anywhere(),
        out_shape=jax.ShapeDtypeStruct(x.shape, x.dtype),
        input_output_aliases={0: 0},
        name="after",
    )(x, *earlier)


def sum_kernel(parts_ref, *refs):
    actives, up_ref, down_ref = refs[:-2], refs[-2], refs[-1]
    groups, _, wide = parts_ref.shape
    width = up_ref.shape[1]
    part = (wide - width) // len(actives)
    up = jnp.zeros(up_ref.shape, F32)
    for group in range(groups):
        up += parts_ref[group, :, :width].astype(F32)
    up_ref[...] = adapter_scale * up
    low = jnp.zeros(down_ref.shape, F32)
    for half, active_ref in enumerate(actives):
        capacity = active_ref.shape[0] // groups
        active = active_ref[...].astype(F32)
        at = width + half * part
        for group in range(groups):
            low += dot(
                parts_ref[group, :, at : at + part][:, :capacity],
                active[group * capacity : (group + 1) * capacity].astype(BF16),
            )
    down_ref[...] = adapter_scale * low


def adapter_gradients(parts, actives, width):
    rank = parts.shape[1]
    return pl.pallas_call(
        sum_kernel,
        in_specs=[vmem()] * (1 + len(actives)),
        out_specs=[vmem()] * 2,
        out_shape=[
            jax.ShapeDtypeStruct((rank, width), F32),
            jax.ShapeDtypeStruct((rank, actives[0].shape[1]), F32),
        ],
        compiler_params=params(),
        name="gradients",
    )(parts, *actives)


def finish_kernel(*refs, groups):
    pieces = refs[:-5]
    probs_ref, ids_ref, names_ref, out_ref, grad_ref = refs[-5:]
    cols = out_ref.shape[1]
    total = pieces[0][:, :cols].astype(F32)
    for ref in pieces[1:]:
        total += ref[:, :cols].astype(F32)
    out_ref[...] = total.astype(BF16)
    dots = []
    for ref in pieces:
        table = ref[:, cols:].astype(F32)
        dots.append(table[:, :groups] + table[:, groups : 2 * groups])
    dots = jnp.concatenate(dots, axis=1)
    probs, ids, names = probs_ref[...], ids_ref[...], names_ref[...]
    picked = [
        jnp.sum(jnp.where(ids[:, k : k + 1] == names, dots, 0.0), axis=1, keepdims=True)
        for k in range(ids.shape[1])
    ]
    picked = jnp.concatenate(picked, axis=1)
    grad = probs * (picked - jnp.sum(probs * picked, axis=1, keepdims=True))
    rest = jnp.zeros((grad.shape[0], 128 - grad.shape[1]), F32)
    grad_ref[...] = jnp.concatenate([grad, rest], axis=1).T[: grad.shape[1]]


def finish(pieces, probs, ids, names, groups, earlier):
    tokens = probs.shape[0]
    count = len(pieces) + 3
    return pl.pallas_call(
        lambda *refs: finish_kernel(*refs[:count], *refs[-2:], groups=groups),
        in_specs=[vmem()] * count + [anywhere()],
        out_specs=[vmem()] * 2,
        out_shape=[
            jax.ShapeDtypeStruct((tokens, pieces[0].shape[1] - 128), BF16),
            jax.ShapeDtypeStruct(probs.shape[::-1], F32),
        ],
        compiler_params=params(40),
        name="finish",
    )(*pieces, probs, ids, names, earlier)


def shards(
    queries,
    keys,
    values,
    document_index,
    residual,
    output_projection,
    norm_gain_weight,
    routed_experts,
    router_logits,
    gate_weight,
    up_weight,
    down_weight,
    adapter_down,
    adapter_up,
    cotangent,
):
    seq_devices = lax.axis_size("seq")
    columns = lax.axis_size("expert")
    column = lax.axis_index("expert")
    place = lax.axis_index("seq")
    tokens = queries.shape[1]
    width = queries.shape[2]
    experts = seq_devices * columns
    rank = adapter_up.shape[1]
    near = columns * tokens
    block = width // columns

    kv_own = jnp.concatenate([keys[0], values[0]], axis=1)
    kv_own = jnp.broadcast_to(kv_own[None], (seq_devices,) + kv_own.shape)
    kv_all = swap(kv_own).reshape(seq_devices * tokens, -1)
    share = output_projection.shape[0] // seq_devices
    pair_share = after(
        lax.dynamic_slice_in_dim(output_projection, place * share, share, 0), kv_own
    )
    pair_share = from_plane(pair_share, 1)
    gate_probs = jax.nn.softmax(router_logits[0].T, axis=0)
    routing = jnp.concatenate([gate_probs, routed_experts[0].T.astype(F32)], axis=0)
    gate_probs = gate_probs.T
    residuals = [
        pack(
            jnp.concatenate(
                [columns_of(residual[0], r, block), columns_of(residual[0], r + 1, block)], 1
            ),
            routing,
        )
        for r in range(0, columns, 2)
    ]
    residuals = [residuals[0]] + [
        from_plane(after(residuals[r // 2], kv_own), r) for r in range(2, columns, 2)
    ]
    pair_share = jnp.broadcast_to(pair_share[None], (seq_devices,) + pair_share.shape)
    attended = attend(queries[0], kv_all, document_index[0], (pair_share,))
    pair_projection = swap(after(pair_share, attended, *residuals[1:]))
    pair_projection = pair_projection.reshape(-1, block)
    attended = [attended] + [from_plane(attended, r) for r in range(2, columns, 2)]

    gain = norm_gain_weight[None]
    scaled = project(
        attended,
        residuals,
        output_projection,
        pair_projection,
        jnp.concatenate([columns_of(gain, 0, block), columns_of(gain, 1, block)], 1),
    )
    capacity = columns // 2 * (9 * tokens * PICKS_PER_TOKEN // (8 * experts))
    crossed = all_planes(scaled)
    upstream = all_planes(later(cotangent[0], crossed[-1]))
    near = columns // 2 * tokens
    slots = []
    for half in range(2):
        if half == 0:
            blocks = residuals
            places = [(i, tokens, 0) for i in range(columns // 2)]
        else:
            blocks = [crossed[1]]
            places = [tile_place(2 * i, 2 * block) for i in range(columns // 2)]
            places = [(0, near + row, lane) for row, lane in places]
        slots.append(
            route(
                column, blocks, places, seq_devices, capacity, tokens, PICKS_PER_TOKEN, columns
            )
        )
    def to_experts(half, first, rest, earlier):
        blocks = crossed[half::2] if rest else [crossed[half]]
        places = slots[half][0]
        return pick(column ^ half, places, blocks, capacity, first, rest, earlier)

    parts = [swap(to_experts(0, True, False, ()))]
    up_factors = later(adapter_up[0], parts[0])
    up_factors = [up_factors] + [from_place(up_factors, r) for r in range(2, seq_devices, 2)]
    picked = to_experts(0, False, True, (*up_factors[1:], crossed[1]))
    parts.append(swap(picked))
    other = [swap(to_experts(1, True, True, (picked,)))]
    up_factors += [from_place(x, 1) for x in up_factors]
    made = [
        expert(
            column // 2,
            x,
            2 * block,
            gate_weight[0],
            up_weight[0],
            adapter_down[0],
            down_weight[0],
            adapter_up[0],
        )
        for x in (parts, other)
    ]
    halves = [(slots[half][0], slots[half][1], upstream[half::2]) for half in range(2)]

    filled = [
        fill(places, gates, cotangents, capacity, (made[1][0],))
        for places, gates, cotangents in halves
    ]
    backs, pieces, earlier = [], {}, ()
    for half, (places, gates, cotangents) in enumerate(halves):
        earlier_sent = [x[0] for x in filled] if half else halves[0][2][1:]
        sent = after(made[half][1], *earlier_sent)
        backs.append(swap(sent))
        rows, weights = filled[half]
        sums = combine(backs[half], weights, rows, places, columns // 2, earlier)
        planes = range(half, columns, 2)
        pieces.update({r: from_plane(x, r) if r else x for r, x in zip(planes, sums)})
        earlier = tuple(pieces[r] for r in planes if r)

    back_slots = back_slots_of(place, up_factors, halves, capacity, pieces[0])
    parts = gradient_parts(
        back_slots,
        [(back, fills[1], half[2]) for back, fills, half in zip(backs, filled, halves)],
        sums[0],
    )
    up_factor_gradient, down_factor_gradient = adapter_gradients(
        swap(parts), [x[0] for x in made], width
    )

    names = (
        jnp.arange(seq_devices)[None, :] * columns
        + (column ^ jnp.arange(columns, dtype=jnp.int32))[:, None]
    )
    combined_output, router_logit_gradient = finish(
        [pieces[r] for r in range(columns)],
        gate_probs,
        routed_experts[0],
        names.reshape(1, experts),
        seq_devices,
        up_factor_gradient,
    )
    return (
        combined_output[None],
        down_factor_gradient.T[None],
        up_factor_gradient[None],
        router_logit_gradient.T[None],
    )


def solution(mesh):
    return jax.shard_map(
        shards,
        mesh=mesh,
        in_specs=(
            P(("groups", "expert"), "seq", None),
            P(("groups", "expert"), "seq", None),
            P(("groups", "expert"), "seq", None),
            P(("groups", "expert"), None),
            P(("groups", "expert"), "seq", None),
            P(None, "expert"),
            P(),
            P(("groups", "expert"), "seq", None),
            P(("groups", "expert"), "seq", None),
            P(("seq", "expert"), None, None),
            P(("seq", "expert"), None, None),
            P(("seq", "expert"), None, None),
            P(("seq", "expert"), None, None),
            P(("seq", "expert"), None, None),
            P(("groups", "expert"), "seq", None),
        ),
        out_specs=(
            P(("groups", "expert"), "seq", None),
            P(("groups", "seq", "expert"), None, None),
            P(("groups", "seq", "expert"), None, None),
            P(("groups", "expert"), "seq", None),
        ),
        check_vma=False,
    )
```

```python
import math

import jax
import jax.numpy as jnp
from jax import lax
from jax.experimental import pallas as pl
from jax.experimental.pallas import tpu as pltpu
from jax.sharding import PartitionSpec as P

QUERY_HEADS = 16
KEY_VALUE_HEADS = 2
HEAD_SIZE = 128
PICKS_PER_TOKEN = 8

adapter_scale = 2.0
norm_eps = 1e-06
BF16 = jnp.bfloat16
F32 = jnp.float32


def dot(a, b):
    return jnp.dot(a, b, preferred_element_type=F32)


def dot_t(a, b):
    return lax.dot_general(a, b, (((1,), (1,)), ((), ())), preferred_element_type=F32)


def attend_kernel(start_ref, query_ref, kv_ref, bias_ref, *refs):
    out_ref = refs[-1]
    tokens = query_ref.shape[0]
    window = bias_ref.shape[1]
    start = pl.multiple_of(start_ref[0] * tokens, tokens)
    bias = bias_ref[...]
    group = QUERY_HEADS // KEY_VALUE_HEADS
    width = KEY_VALUE_HEADS * HEAD_SIZE
    factor = math.log2(math.e) / math.sqrt(HEAD_SIZE)
    for kv_head in range(KEY_VALUE_HEADS):
        first = kv_head * HEAD_SIZE
        key_rows = kv_ref[pl.ds(start, window), first : first + HEAD_SIZE]
        value_rows = kv_ref[pl.ds(start, window), width + first : width + first + HEAD_SIZE]
        for pair in range(group // 2):
            at = (kv_head * group + pair * 2) * HEAD_SIZE
            rows = jnp.concatenate(
                [
                    query_ref[:, at : at + HEAD_SIZE],
                    query_ref[:, at + HEAD_SIZE : at + 2 * HEAD_SIZE],
                ],
                axis=0,
            )
            scores = dot_t(rows, key_rows).reshape(2, tokens, window) + bias[None]
            highest = jnp.max(scores, axis=-1, keepdims=True)
            raised = jnp.exp2((scores - highest) * factor)
            total = jnp.sum(raised, axis=-1, keepdims=True)
            mixed = dot(raised.astype(BF16).reshape(2 * tokens, window), value_rows)
            mixed = (mixed.reshape(2, tokens, HEAD_SIZE) / total).astype(BF16)
            out_ref[:, at : at + HEAD_SIZE] = mixed[0]
            out_ref[:, at + HEAD_SIZE : at + 2 * HEAD_SIZE] = mixed[1]


def attend(queries, kv_all, documents, earlier):
    tokens = queries.shape[0]
    length = kv_all.shape[0]
    place = lax.axis_index("seq")
    window = min(length, length // 2 + tokens)
    first_block = jnp.clip(place + 1 - window // tokens, 0, (length - window) // tokens)
    mine = place * tokens + jnp.arange(tokens)
    there = first_block * tokens + jnp.arange(window)
    doc_mine = lax.dynamic_slice_in_dim(documents, place * tokens, tokens)
    doc_there = lax.dynamic_slice_in_dim(documents, first_block * tokens, window)
    allowed = (there[None, :] <= mine[:, None]) & (doc_there[None, :] == doc_mine[:, None])
    bias = jnp.where(allowed, 0.0, -jnp.inf).astype(F32)
    return pl.pallas_call(
        attend_kernel,
        out_shape=jax.ShapeDtypeStruct(queries.shape, BF16),
        in_specs=[
            pl.BlockSpec(memory_space=pltpu.SMEM),
            pl.BlockSpec(memory_space=pltpu.VMEM),
            pl.BlockSpec(memory_space=pltpu.VMEM),
            pl.BlockSpec(memory_space=pltpu.VMEM),
        ]
        + [anywhere()] * len(earlier),
        out_specs=pl.BlockSpec(memory_space=pltpu.VMEM),
        compiler_params=params(),
        name="attend",
    )(first_block.reshape(1).astype(jnp.int32), queries, kv_all, bias, *earlier)


def vmem():
    return pl.BlockSpec(memory_space=pltpu.VMEM)


def anywhere():
    return pl.BlockSpec(memory_space=pl.ANY)


def smem():
    return pl.BlockSpec(memory_space=pltpu.SMEM)


def params(mebibytes=24):
    return pltpu.CompilerParams(vmem_limit_bytes=mebibytes << 20)


def cost(flops, bytes_accessed):
    return pl.CostEstimate(flops=flops, bytes_accessed=bytes_accessed, transcendentals=0)


def pack_kernel(residual_ref, routing_ref, out_ref):
    tokens = residual_ref.shape[0]
    out_ref[:tokens, :] = residual_ref[...]
    routing = routing_ref[...]
    picks = routing.shape[0] // 2
    gates = routing[:picks].astype(BF16).astype(F32)
    table = jnp.concatenate(
        [
            jnp.concatenate([gates, routing[:picks] - gates], axis=0),
            jnp.concatenate([routing[picks:], jnp.zeros((picks, tokens), F32)], axis=0),
        ],
        axis=1,
    )
    wide = table.shape[1]
    out_ref[tokens:, :wide] = table.astype(BF16)
    if wide < out_ref.shape[1]:
        out_ref[tokens:, wide:] = jnp.zeros((16, out_ref.shape[1] - wide), BF16)


def pack(residual, routing):
    tokens, cols = residual.shape
    return pl.pallas_call(
        pack_kernel,
        in_specs=[vmem()] * 2,
        out_specs=vmem(),
        out_shape=jax.ShapeDtypeStruct((tokens + 16, cols), BF16),
        compiler_params=params(),
        name="pack",
    )(residual, routing)


def tile_place(number, cols):
    across = cols // 128
    return number // across * 16, number % across * 128


def project_kernel(*refs, blocks):
    attended, residuals = refs[:blocks], refs[blocks : 2 * blocks]
    own_ref, pair_ref, gain_ref, out_ref = refs[2 * blocks :]
    cols = own_ref.shape[1]
    tokens = attended[0].shape[0]
    near = blocks * tokens
    rows = jnp.concatenate([ref[...] for ref in attended], axis=0)
    square = None
    for side, weight_ref in enumerate((own_ref, pair_ref)):
        at = side * cols
        stream = dot(rows, weight_ref[...])
        stream += jnp.concatenate(
            [ref[:tokens, at : at + cols] for ref in residuals], axis=0
        ).astype(F32)
        out_ref[:near, at : at + cols] = (stream * gain_ref[:, at : at + cols]).astype(BF16)
        for lane in range(0, cols, 128):
            piece = stream[:, lane : lane + 128]
            square = piece * piece if square is None else square + piece * piece
    square = jnp.sum(square.T, axis=0, keepdims=True)
    square = jnp.concatenate(
        [square[:, i * tokens : (i + 1) * tokens] for i in range(blocks)], axis=0
    )
    high = square.astype(BF16).astype(F32)
    rest = jnp.zeros((8 - blocks, tokens), F32)
    out_ref[near:, :] = jnp.zeros((out_ref.shape[0] - near, 2 * cols), BF16)
    for i, ref in enumerate(residuals):
        row, lane = tile_place(2 * i, 2 * cols)
        out_ref[near + row : near + row + 16, lane : lane + 2 * tokens] = ref[
            tokens:, : 2 * tokens
        ]
    row, lane = tile_place(2 * blocks, 2 * cols)
    out_ref[near + row : near + row + 16, lane : lane + tokens] = jnp.concatenate(
        [high, rest, square - high, rest], axis=0
    ).astype(BF16)


def project(attended, residuals, own_weight, pair_weight, gain):
    blocks = len(attended)
    tokens, width = attended[0].shape
    cols = own_weight.shape[1]
    rows = blocks * tokens
    more = tile_place(2 * blocks, 2 * cols)[0] + 16
    return pl.pallas_call(
        lambda *refs: project_kernel(*refs, blocks=blocks),
        in_specs=[vmem()] * (2 * blocks + 3),
        out_specs=vmem(),
        out_shape=jax.ShapeDtypeStruct((rows + more, 2 * cols), BF16),
        compiler_params=params(),
        cost_estimate=cost(4 * rows * width * cols, 4 * width * cols),
        name="project",
    )(*attended, *residuals, own_weight, pair_weight, gain.reshape(1, 2 * cols))


def hits_of(slots, capacity):
    groups, near = slots.shape
    places = lax.broadcasted_iota(jnp.int32, (capacity, near), 0)
    return jnp.concatenate(
        [
            jnp.where(places == slots[group : group + 1, :], 1.0, 0.0).astype(F32)
            for group in range(groups)
        ],
        axis=0,
    )


def route_kernel(column_ref, *refs, places, capacity, picks, columns):
    blocks, slot_ref, gate_ref = refs[:-2], refs[-2], refs[-1]
    groups, near = slot_ref.shape
    tokens = near // len(places)
    tables = [
        blocks[number][row : row + 16, lane : lane + 2 * tokens].astype(F32)
        for number, row, lane in places
    ]
    probs = jnp.concatenate([x[:, :tokens] for x in tables], axis=1)
    probs = probs[:picks] + probs[picks : 2 * picks]
    ids = jnp.concatenate([x[:picks, tokens:] for x in tables], axis=1).astype(jnp.int32)
    member, gates = [], []
    for group in range(groups):
        hit = ids == group * columns + column_ref[0]
        member.append(jnp.sum(hit.astype(F32), axis=0, keepdims=True))
        gates.append(jnp.sum(jnp.where(hit, probs, 0.0), axis=0, keepdims=True))
    member = jnp.concatenate(member, axis=0)
    earlier = lax.broadcasted_iota(jnp.int32, (near, near), 0) < lax.broadcasted_iota(
        jnp.int32, (near, near), 1
    )
    ranks = dot(member.astype(BF16), earlier.astype(BF16)).astype(jnp.int32)
    slot_ref[...] = jnp.where(member > 0.0, ranks, capacity)
    gate_ref[...] = jnp.concatenate(gates, axis=0)


def route(column, blocks, places, groups, capacity, tokens, picks, columns):
    near = len(places) * tokens
    return pl.pallas_call(
        lambda *refs: route_kernel(
            *refs, places=places, capacity=capacity, picks=picks, columns=columns
        ),
        in_specs=[smem()] + [vmem()] * len(blocks),
        out_specs=[vmem()] * 2,
        out_shape=[
            jax.ShapeDtypeStruct((groups, near), jnp.int32),
            jax.ShapeDtypeStruct((groups, near), F32),
        ],
        compiler_params=params(),
        name="route",
    )(column.reshape(1), *blocks)


def place_sides(out_ref, picked, at, first):
    half = picked.shape[1] // 2
    for side in range(2):
        lane = pl.multiple_of(at + ((first ^ side) % 2) * half, 128)
        out_ref[:, pl.ds(lane, half)] = picked[:, side * half : (side + 1) * half]


def pick_kernel(first_ref, slot_ref, *refs, count, capacity, first, rest):
    blocks, out_ref = refs[:count], refs[-1]
    near = slot_ref.shape[1]
    hits = hits_of(slot_ref[...], capacity)
    places = hits.astype(BF16)
    cols = blocks[0].shape[1]
    skip = 0 if first else cols
    if first:
        picked = dot(places, blocks[0][:near, :]).astype(BF16)
        place_sides(out_ref, picked, 0, first_ref[0])
    if not rest:
        return
    tokens = near // count
    row, lane = tile_place(2 * count, cols)
    squares = [
        x[near + row : near + row + 16, lane : lane + tokens].astype(F32) for x in blocks
    ]
    inverses = []
    for b in range(count):
        total = jnp.zeros((1, tokens), F32)
        for i in range(count):
            total += squares[i][i ^ b : (i ^ b) + 1] + squares[i][8 + (i ^ b) : 9 + (i ^ b)]
        inverses.append(lax.rsqrt(total / (count * cols) + norm_eps))
    factors = jnp.sum(hits * jnp.concatenate(inverses, axis=1), axis=1, keepdims=True)
    for i in range(1, count):
        rows = jnp.concatenate(
            [blocks[i][(i ^ b) * tokens : ((i ^ b) + 1) * tokens, :] for b in range(count)], axis=0
        )
        place_sides(out_ref, dot(places, rows).astype(BF16), i * cols - skip, first_ref[0])
    high = factors.astype(BF16).astype(F32)
    lanes = lax.broadcasted_iota(jnp.int32, (factors.shape[0], 128), 1)
    table = jnp.where(lanes == 0, high, jnp.where(lanes == 1, factors - high, 0.0))
    out_ref[:, count * cols - skip :] = table.astype(BF16)


def pick(plane, slots, blocks, capacity, first, rest, earlier):
    groups, near = slots.shape
    count = len(blocks)
    rows, cols = groups * capacity, blocks[0].shape[1]
    wide = (cols if first else 0) + ((count - 1) * cols + 128 if rest else 0)
    return pl.pallas_call(
        lambda *refs: pick_kernel(
            *refs[: 2 + count],
            refs[-1],
            count=count,
            capacity=capacity,
            first=first,
            rest=rest,
        ),
        in_specs=[smem()] + [vmem()] * (1 + count) + [anywhere()] * len(earlier),
        out_specs=vmem(),
        out_shape=jax.ShapeDtypeStruct((rows, wide), BF16),
        compiler_params=params(),
        cost_estimate=cost(2 * rows * near * wide, 2 * rows * wide),
        name="pick",
    )(plane.reshape(1), slots, *blocks, *earlier)


def fill_kernel(slot_ref, gate_ref, *refs, capacity):
    blocks, out_ref, weight_ref = refs[:-2], refs[-2], refs[-1]
    rows = jnp.concatenate([block[...] for block in blocks], axis=0)
    hits = hits_of(slot_ref[...], capacity)
    out_ref[...] = dot(hits.astype(BF16), rows).astype(BF16)
    count, near = hits.shape
    gates = [
        hits[group * capacity : (group + 1) * capacity] * gate_ref[group : group + 1, :]
        for group in range(gate_ref.shape[0])
    ]
    if count % 128:
        gates.append(jnp.zeros((-count % 128, near), F32))
    weight_ref[...] = jnp.concatenate(gates, axis=0).T[:, :count].astype(BF16)


def fill(slots, gates, blocks, capacity, earlier):
    groups, near = slots.shape
    rows, cols = groups * capacity, blocks[0].shape[1]
    return pl.pallas_call(
        lambda *refs: fill_kernel(*refs[: 2 + len(blocks)], *refs[-2:], capacity=capacity),
        in_specs=[vmem()] * (2 + len(blocks)) + [anywhere()] * len(earlier),
        out_specs=[vmem()] * 2,
        out_shape=[
            jax.ShapeDtypeStruct((rows, cols), BF16),
            jax.ShapeDtypeStruct((near, rows), BF16),
        ],
        compiler_params=params(),
        cost_estimate=cost(2 * rows * near * cols, 2 * rows * cols),
        name="fill",
    )(slots, gates, *blocks, *earlier)


def back_kernel(place_ref, *refs, capacity, count):
    out_ref, made_ref = refs[-2:]
    groups, rank, wide = out_ref.shape
    factors = jnp.concatenate([ref[...] for ref in refs[:groups]], axis=0)
    refs = refs[groups:]
    halves = 2
    part = wide // halves
    out_ref[...] = jnp.zeros(out_ref.shape, BF16)
    for half in range(halves):
        slot_ref, gate_ref, *blocks = refs[half * (2 + count) : (half + 1) * (2 + count)]
        rows = jnp.concatenate([block[...] for block in blocks], axis=0)
        made_ref[...] = dot_t(factors, rows)
        hits = hits_of(slot_ref[...], capacity)
        for group in range(groups):
            x = place_ref[0] ^ group
            at = pl.multiple_of((x // 2 + x % 2 * (groups // 2)) * rank, rank)
            mine = made_ref[pl.ds(at, rank), :] * gate_ref[group : group + 1, :]
            slots = hits[group * capacity : (group + 1) * capacity].astype(BF16)
            out_ref[group, :, half * part : half * part + capacity] = dot_t(
                mine.astype(BF16), slots
            ).astype(BF16)


def back_slots_of(place, factors, halves, capacity, earlier):
    operands = [x for slots, gates, blocks in halves for x in (slots, gates, *blocks)]
    count = len(halves[0][2])
    groups, near = halves[0][0].shape
    rank, width = factors[0].shape
    part = capacity + -capacity % 128
    return pl.pallas_call(
        lambda *refs: back_kernel(
            *refs[: 1 + groups + len(operands)], *refs[-2:], capacity=capacity, count=count
        ),
        in_specs=[smem()] + [vmem()] * (groups + len(operands)) + [anywhere()],
        out_specs=vmem(),
        out_shape=jax.ShapeDtypeStruct((groups, rank, 2 * part), BF16),
        compiler_params=params(),
        scratch_shapes=[pltpu.VMEM((groups * rank, near), F32)],
        cost_estimate=cost(4 * near * groups * rank * width, 4 * groups * rank * width),
        name="back_low",
    )(place.reshape(1), *factors, *operands, earlier)


def gradient_kernel(back_ref, *refs, count, rank):
    out_ref = refs[-1]
    groups = back_ref.shape[0]
    made = 0.0
    for half in range(2):
        low_ref, weight_ref, *blocks = refs[half * (2 + count) : (half + 1) * (2 + count)]
        rows = jnp.concatenate([block[...] for block in blocks], axis=0)
        low = low_ref[...].astype(F32)
        slots = low.shape[0]
        if slots % 128:
            low = jnp.concatenate([low, jnp.zeros((-slots % 128, low.shape[1]), F32)], axis=0)
        low = low.T[:rank, :slots]
        low = jnp.concatenate([low] * groups, axis=0)
        capacity = slots // groups
        group = lax.broadcasted_iota(jnp.int32, low.shape, 0) // rank
        place = lax.broadcasted_iota(jnp.int32, low.shape, 1) - group * capacity
        low = jnp.where((place >= 0) & (place < capacity), low, 0.0).astype(BF16)
        made += dot(dot_t(low, weight_ref[...]).astype(BF16), rows)
    width = made.shape[1]
    out_ref[:, :, :width] = made.astype(BF16).reshape(groups, rank, width)
    out_ref[:, :, width:] = back_ref[...]


def gradient_parts(back_slots, halves, earlier):
    groups, rank, wide = back_slots.shape
    width = halves[0][2][0].shape[1]
    count = len(halves[0][2])
    near = halves[0][1].shape[0]
    operands, in_specs = [back_slots], [pl.BlockSpec(back_slots.shape, lambda i: (0, 0, 0))]
    for back, weights, blocks in halves:
        operands += [back, weights, *blocks]
        in_specs.append(pl.BlockSpec((back.shape[0], 128), lambda i: (0, width // 128)))
        in_specs += [pl.BlockSpec(x.shape, lambda i: (0, 0)) for x in (weights, *blocks)]
    return pl.pallas_call(
        lambda *refs: gradient_kernel(*refs[: len(operands)], refs[-1], count=count, rank=rank),
        grid=(1,),
        in_specs=in_specs + [anywhere()],
        out_specs=pl.BlockSpec((groups, rank, width + wide), lambda i: (0, 0, 0)),
        out_shape=jax.ShapeDtypeStruct((groups, rank, width + wide), BF16),
        compiler_params=params(56),
        cost_estimate=cost(4 * near * groups * rank * width, 4 * near * width),
        name="gradient",
    )(*operands, earlier)


def expert_kernel(
    pair_ref,
    *refs,
    cols,
):
    *parts, gate_ref, up_ref, factor_ref, down_ref, up_factor_ref, out_active, out_ref = refs
    more_ref = parts[-1]
    skip = cols if len(parts) > 1 else 0
    gate = up = 0.0
    for i in range(gate_ref.shape[0] // cols):
        if i == 0:
            rows = parts[0][:, :cols]
        else:
            rows = more_ref[:, i * cols - skip : (i + 1) * cols - skip]
        at = pl.ds(pl.multiple_of((pair_ref[0] ^ i) * cols, cols), cols)
        gate += dot(rows, gate_ref[at, :])
        up += dot(rows, up_ref[at, :])
    norm = more_ref[:, more_ref.shape[1] - 128 :].astype(F32)
    norm = norm[:, :1] + norm[:, 1:2]
    gate, up = gate * norm, up * norm
    active = (gate / (1.0 + jnp.exp(-gate)) * up).astype(BF16)
    out_active[...] = active
    low = dot(active, factor_ref[...]).astype(BF16)
    made = dot(active, down_ref[...]) + adapter_scale * dot(low, up_factor_ref[...])
    cols, rank = made.shape[1], low.shape[1]
    out_ref[:, :cols] = made.astype(BF16)
    out_ref[:, cols:] = jnp.zeros((made.shape[0], out_ref.shape[1] - cols), BF16)
    out_ref[:, cols : cols + rank] = low


def expert(pair, parts, cols, gate_weight, up_weight, factor, down_weight, up_factor):
    count = parts[0].shape[0]
    width, units = gate_weight.shape
    step = count // 2

    def whole(x):
        return pl.BlockSpec(x.shape, lambda i: (0, 0))

    weights = (gate_weight, up_weight, factor, down_weight, up_factor)
    return pl.pallas_call(
        lambda *refs: expert_kernel(*refs, cols=cols),
        grid=(count // step,),
        in_specs=[smem()]
        + [pl.BlockSpec((step, x.shape[1]), lambda i: (i, 0)) for x in parts]
        + [whole(x) for x in weights],
        out_specs=[
            pl.BlockSpec((step, units), lambda i: (i, 0)),
            pl.BlockSpec((step, width + 128), lambda i: (i, 0)),
        ],
        out_shape=[
            jax.ShapeDtypeStruct((count, units), BF16),
            jax.ShapeDtypeStruct((count, width + 128), BF16),
        ],
        compiler_params=params(50),
        cost_estimate=cost(0, 0),
        name="expert",
    )(pair.reshape(1), *parts, *weights)


def combine_kernel(back_ref, weight_ref, upstream_ref, slot_ref, *outs):
    blocks = len(outs)
    cols = upstream_ref.shape[1]
    groups, near = slot_ref.shape
    tokens = near // blocks
    back = back_ref[:, :cols]
    dots = jnp.sum(back.astype(F32) * upstream_ref[...].astype(F32), axis=1, keepdims=True)
    total = dot(weight_ref[...], back).astype(BF16)
    capacity = back.shape[0] // groups
    places = lax.broadcasted_iota(jnp.int32, (capacity, near), 0)
    found = []
    for group in range(groups):
        mine = dots[group * capacity : (group + 1) * capacity]
        hits = places == slot_ref[group : group + 1, :]
        found.append(jnp.sum(jnp.where(hits, mine, 0.0), axis=0, keepdims=True))
    found = jnp.concatenate(found, axis=0)
    high = found.astype(BF16).astype(F32)
    rest = jnp.zeros((128 - 2 * groups, near), F32)
    table = jnp.concatenate([high, found - high, rest], axis=0).T.astype(BF16)
    for block in range(blocks):
        outs[block][:, :cols] = total[block * tokens : (block + 1) * tokens]
        outs[block][:, cols:] = table[block * tokens : (block + 1) * tokens]


def combine(back, weights, upstream, slots, blocks, earlier):
    rows, cols = upstream.shape
    near = weights.shape[0]
    return pl.pallas_call(
        lambda *refs: combine_kernel(*refs[:4], *refs[4 + len(earlier) :]),
        in_specs=[vmem()] * 4 + [anywhere()] * len(earlier),
        out_specs=[vmem()] * blocks,
        out_shape=[jax.ShapeDtypeStruct((near // blocks, cols + 128), BF16)] * blocks,
        compiler_params=params(40),
        cost_estimate=cost(2 * rows * near * cols, 2 * cols * (rows + near)),
        name="combine",
    )(back, weights, upstream, slots, *earlier)


def from_plane(x, r):
    size = lax.axis_size("expert")
    return lax.ppermute(x, "expert", [(i, i ^ r) for i in range(size)])


def from_place(x, r):
    size = lax.axis_size("seq")
    return lax.ppermute(x, "seq", [(i, i ^ r) for i in range(size)])


def copy_kernel(x_ref, *refs):
    refs[-1][...] = x_ref[...]


def later(x, *earlier):
    return pl.pallas_call(
        copy_kernel,
        in_specs=[vmem()] + [anywhere()] * len(earlier),
        out_specs=vmem(),
        out_shape=jax.ShapeDtypeStruct(x.shape, x.dtype),
        compiler_params=params(),
        name="later",
    )(x, *earlier)


def all_planes(x):
    found = [x, from_plane(x, 1)]
    for r in range(2, lax.axis_size("expert"), 2):
        found.append(from_plane(x, r))
        found.append(from_plane(found[-1], 1))
    return found


def columns_of(x, r, size):
    return lax.dynamic_slice_in_dim(x, (lax.axis_index("expert") ^ r) * size, size, 1)


def swap(x):
    return lax.all_to_all(x, "seq", split_axis=0, concat_axis=0, tiled=True)


def after(x, *earlier):
    return pl.pallas_call(
        lambda *refs: None,
        in_specs=[anywhere()] * (1 + len(earlier)),
        out_specs=anywhere(),
        out_shape=jax.ShapeDtypeStruct(x.shape, x.dtype),
        input_output_aliases={0: 0},
        name="after",
    )(x, *earlier)


def sum_kernel(parts_ref, *refs):
    actives, up_ref, down_ref = refs[:-2], refs[-2], refs[-1]
    groups, _, wide = parts_ref.shape
    width = up_ref.shape[1]
    part = (wide - width) // len(actives)
    up = jnp.zeros(up_ref.shape, F32)
    for group in range(groups):
        up += parts_ref[group, :, :width].astype(F32)
    up_ref[...] = adapter_scale * up
    low = jnp.zeros(down_ref.shape, F32)
    for half, active_ref in enumerate(actives):
        capacity = active_ref.shape[0] // groups
        active = active_ref[...].astype(F32)
        at = width + half * part
        for group in range(groups):
            low += dot(
                parts_ref[group, :, at : at + part][:, :capacity],
                active[group * capacity : (group + 1) * capacity].astype(BF16),
            )
    down_ref[...] = adapter_scale * low


def adapter_gradients(parts, actives, width):
    rank = parts.shape[1]
    return pl.pallas_call(
        sum_kernel,
        in_specs=[vmem()] * (1 + len(actives)),
        out_specs=[vmem()] * 2,
        out_shape=[
            jax.ShapeDtypeStruct((rank, width), F32),
            jax.ShapeDtypeStruct((rank, actives[0].shape[1]), F32),
        ],
        compiler_params=params(56),
        name="gradients",
    )(parts, *actives)


def finish_kernel(*refs, groups):
    pieces = refs[:-5]
    probs_ref, ids_ref, names_ref, out_ref, grad_ref = refs[-5:]
    cols = out_ref.shape[1]
    total = pieces[0][:, :cols].astype(F32)
    for ref in pieces[1:]:
        total += ref[:, :cols].astype(F32)
    out_ref[...] = total.astype(BF16)
    dots = []
    for ref in pieces:
        table = ref[:, cols:].astype(F32)
        dots.append(table[:, :groups] + table[:, groups : 2 * groups])
    dots = jnp.concatenate(dots, axis=1)
    probs, ids, names = probs_ref[...], ids_ref[...], names_ref[...]
    picked = [
        jnp.sum(jnp.where(ids[:, k : k + 1] == names, dots, 0.0), axis=1, keepdims=True)
        for k in range(ids.shape[1])
    ]
    picked = jnp.concatenate(picked, axis=1)
    grad = probs * (picked - jnp.sum(probs * picked, axis=1, keepdims=True))
    rest = jnp.zeros((grad.shape[0], 128 - grad.shape[1]), F32)
    grad_ref[...] = jnp.concatenate([grad, rest], axis=1).T[: grad.shape[1]]


def finish(pieces, probs, ids, names, groups, earlier):
    tokens = probs.shape[0]
    count = len(pieces) + 3
    return pl.pallas_call(
        lambda *refs: finish_kernel(*refs[:count], *refs[-2:], groups=groups),
        in_specs=[vmem()] * count + [anywhere()],
        out_specs=[vmem()] * 2,
        out_shape=[
            jax.ShapeDtypeStruct((tokens, pieces[0].shape[1] - 128), BF16),
            jax.ShapeDtypeStruct(probs.shape[::-1], F32),
        ],
        compiler_params=params(40),
        name="finish",
    )(*pieces, probs, ids, names, earlier)


def shards(
    queries,
    keys,
    values,
    document_index,
    residual,
    output_projection,
    norm_gain_weight,
    routed_experts,
    router_logits,
    gate_weight,
    up_weight,
    down_weight,
    adapter_down,
    adapter_up,
    cotangent,
):
    seq_devices = lax.axis_size("seq")
    columns = lax.axis_size("expert")
    column = lax.axis_index("expert")
    place = lax.axis_index("seq")
    tokens = queries.shape[1]
    width = queries.shape[2]
    experts = seq_devices * columns
    rank = adapter_up.shape[1]
    near = columns * tokens
    block = width // columns

    kv_own = jnp.concatenate([keys[0], values[0]], axis=1)
    kv_own = jnp.broadcast_to(kv_own[None], (seq_devices,) + kv_own.shape)
    kv_all = swap(kv_own).reshape(seq_devices * tokens, -1)
    share = output_projection.shape[0] // seq_devices
    pair_share = after(
        lax.dynamic_slice_in_dim(output_projection, place * share, share, 0), kv_own
    )
    pair_share = from_plane(pair_share, 1)
    gate_probs = jax.nn.softmax(router_logits[0].T, axis=0)
    routing = jnp.concatenate([gate_probs, routed_experts[0].T.astype(F32)], axis=0)
    gate_probs = gate_probs.T
    residuals = [
        pack(
            jnp.concatenate(
                [columns_of(residual[0], r, block), columns_of(residual[0], r + 1, block)], 1
            ),
            routing,
        )
        for r in range(0, columns, 2)
    ]
    residuals = [residuals[0]] + [
        from_plane(after(residuals[r // 2], kv_own), r) for r in range(2, columns, 2)
    ]
    pair_share = jnp.broadcast_to(pair_share[None], (seq_devices,) + pair_share.shape)
    attended = attend(queries[0], kv_all, document_index[0], (pair_share,))
    pair_projection = swap(after(pair_share, attended, *residuals[1:]))
    pair_projection = pair_projection.reshape(-1, block)
    attended = [attended] + [from_plane(attended, r) for r in range(2, columns, 2)]

    gain = norm_gain_weight[None]
    scaled = project(
        attended,
        residuals,
        output_projection,
        pair_projection,
        jnp.concatenate([columns_of(gain, 0, block), columns_of(gain, 1, block)], 1),
    )
    capacity = columns // 2 * (9 * tokens * PICKS_PER_TOKEN // (8 * experts))
    crossed = all_planes(scaled)
    upstream = all_planes(later(cotangent[0], crossed[-1]))
    near = columns // 2 * tokens
    slots = []
    for half in range(2):
        if half == 0:
            blocks = residuals
            places = [(i, tokens, 0) for i in range(columns // 2)]
        else:
            blocks = [crossed[1]]
            places = [tile_place(2 * i, 2 * block) for i in range(columns // 2)]
            places = [(0, near + row, lane) for row, lane in places]
        slots.append(
            route(
                column, blocks, places, seq_devices, capacity, tokens, PICKS_PER_TOKEN, columns
            )
        )
    def to_experts(half, first, rest, earlier):
        blocks = crossed[half::2] if rest else [crossed[half]]
        places = slots[half][0]
        return pick(column ^ half, places, blocks, capacity, first, rest, earlier)

    parts = [swap(to_experts(0, True, False, ()))]
    up_factors = later(adapter_up[0], parts[0])
    up_factors = [up_factors] + [from_place(up_factors, r) for r in range(2, seq_devices, 2)]
    picked = to_experts(0, False, True, (*up_factors[1:], crossed[1]))
    parts.append(swap(picked))
    other = [swap(to_experts(1, True, True, (picked,)))]
    up_factors += [from_place(x, 1) for x in up_factors]
    made = [
        expert(
            column // 2,
            x,
            2 * block,
            gate_weight[0],
            up_weight[0],
            adapter_down[0],
            down_weight[0],
            adapter_up[0],
        )
        for x in (parts, other)
    ]
    halves = [(slots[half][0], slots[half][1], upstream[half::2]) for half in range(2)]

    filled = [
        fill(places, gates, cotangents, capacity, (made[1][0],))
        for places, gates, cotangents in halves
    ]
    backs, pieces, earlier = [], {}, ()
    for half, (places, gates, cotangents) in enumerate(halves):
        earlier_sent = [x[0] for x in filled] if half else halves[0][2][1:]
        sent = after(made[half][1], *earlier_sent)
        backs.append(swap(sent))
        rows, weights = filled[half]
        sums = combine(backs[half], weights, rows, places, columns // 2, earlier)
        planes = range(half, columns, 2)
        pieces.update({r: from_plane(x, r) if r else x for r, x in zip(planes, sums)})
        earlier = tuple(pieces[r] for r in planes if r)

    back_slots = back_slots_of(place, up_factors, halves, capacity, pieces[0])
    parts = gradient_parts(
        back_slots,
        [(back, fills[1], half[2]) for back, fills, half in zip(backs, filled, halves)],
        sums[0],
    )
    up_factor_gradient, down_factor_gradient = adapter_gradients(
        swap(parts), [x[0] for x in made], width
    )

    names = (
        jnp.arange(seq_devices)[None, :] * columns
        + (column ^ jnp.arange(columns, dtype=jnp.int32))[:, None]
    )
    combined_output, router_logit_gradient = finish(
        [pieces[r] for r in range(columns)],
        gate_probs,
        routed_experts[0],
        names.reshape(1, experts),
        seq_devices,
        up_factor_gradient,
    )
    return (
        combined_output[None],
        down_factor_gradient.T[None],
        up_factor_gradient[None],
        router_logit_gradient.T[None],
    )


def solution(mesh):
    return jax.shard_map(
        shards,
        mesh=mesh,
        in_specs=(
            P(("groups", "expert"), "seq", None),
            P(("groups", "expert"), "seq", None),
            P(("groups", "expert"), "seq", None),
            P(("groups", "expert"), None),
            P(("groups", "expert"), "seq", None),
            P(None, "expert"),
            P(),
            P(("groups", "expert"), "seq", None),
            P(("groups", "expert"), "seq", None),
            P(("seq", "expert"), None, None),
            P(("seq", "expert"), None, None),
            P(("seq", "expert"), None, None),
            P(("seq", "expert"), None, None),
            P(("seq", "expert"), None, None),
            P(("groups", "expert"), "seq", None),
        ),
        out_specs=(
            P(("groups", "expert"), "seq", None),
            P(("groups", "seq", "expert"), None, None),
            P(("groups", "seq", "expert"), None, None),
            P(("groups", "expert"), "seq", None),
        ),
        check_vma=False,
    )
```
